256 devices in a mesh: row: 32 (over z, x), col: 8 (over y, core).
Axes of the slice: x: 4, y: 4, z: 8, core: 2. Of those that a mesh axis runs over, the one named last changes fastest.
Arguments:
- features: bfloat16 [32768, 128], P(('col', 'row')), may hold values from -6 to 6
- upstream: bfloat16 [32768, 256], P(('col', 'row')), may hold values from -6 to 6
- tile_values: bfloat16 [32, 8, 192, 128, 128], P('row', 'col'), may hold values from -0.046875 to 0.046875
- tile_rows: int32 [32, 8, 192], P('row', 'col'), may hold values from 0 to 7, as said below
- tile_cols: int32 [32, 8, 192], P('row', 'col'), may hold values from 0 to 31, as said below
- tile_count: int32 [32, 8], P('row', 'col'), may hold values from 48 to 192, as said below
- w_one: bfloat16 [128, 256], replicated, may hold values from -0.5 to 0.5
- b_one: float32 [256], replicated, may hold values from -3 to 3
- w_two: bfloat16 [256, 256], replicated, may hold values from -0.375 to 0.375
- b_two: float32 [256], replicated, may hold values from -3 to 3
Outputs:
- hidden_out: bfloat16 [32768, 256], P(('col', 'row'))
- grad_w_one: float32 [128, 256], replicated
- grad_b_one: float32 [256], replicated
- grad_w_two: float32 [256, 256], replicated
- grad_b_two: float32 [256], replicated
The draws below stay inside these ranges and needn't reach their ends.
Inputs may be any that keep to these rules, and one draw needn't show every extreme that they name: Within one block the pairs (tile_rows, tile_cols) of all slots are distinct. `tile_cols`: see tile_rows. `tile_count`: some block has all 192 slots live.
All inputs are finite; a program needn't handle non-finite values.
Results may differ from the reference program's by a relative error of at most 0.024.
Values may be sent and summed in bfloat16 or wider, within the bound.
A program may use at most 128 MiB of HBM per device.

```python
import jax
import jax.numpy as jnp
from jax import lax

F = 128
HID = 256
TILE = 128
ROWS_DEV = 128
NODES = 32768
ROW_TILES = 8
COL_TILES = 32
TILES_DEV = 192
N_ROW = 32
N_COL = 8


def pick_slots(key):
    keys = jax.random.split(key, N_ROW * N_COL)
    chosen = jax.vmap(lambda part_key: jax.random.permutation(part_key, ROW_TILES * COL_TILES)[:TILES_DEV])(keys)
    return chosen.reshape(N_ROW, N_COL, TILES_DEV).astype(jnp.int32)


def draw_tile_rows(key, part):
    return pick_slots(key) // COL_TILES


def draw_tile_cols(key, part):
    return pick_slots(key) % COL_TILES


def draw_tile_count(key, part):
    key = jax.random.fold_in(key, 5)
    counts = jax.random.randint(key, (N_ROW * N_COL,), TILES_DEV // 4, TILES_DEV + 1).astype(jnp.int32)
    filled = jax.random.randint(jax.random.fold_in(key, 1), (), 0, N_ROW * N_COL)
    counts = counts.at[filled].set(TILES_DEV)
    return counts.reshape(N_ROW, N_COL)


def block_levels(own_key, extent, shards, smallest, largest):
    gain = 1.0
    for dim, shards_of in shards:
        steps = jax.random.uniform(jax.random.fold_in(jax.random.fold_in(own_key, 6), dim), (shards_of,), jnp.float32, smallest / len(shards), largest / len(shards))
        gain = gain * jnp.repeat(jnp.exp(steps), extent[dim] // shards_of).reshape((-1,) + (1,) * (len(extent) - 1 - dim))
    return gain


def centred(own_key, extent, spread, reach, shards=(), kind=jnp.bfloat16):
    loudness = block_levels(own_key, extent, shards, -0.22, 0.18) if shards else 1.0
    array = jax.random.normal(own_key, extent, jnp.float32) * spread * loudness
    return jnp.minimum(jnp.maximum(array, -reach), reach).astype(kind)


def setup_inputs(seed: int = 0) -> dict:
    arg_keys = jax.random.split(jax.random.key(seed), 11)
    features = centred(arg_keys[0], (NODES, F), 1.0, 6.0, ((0, 256),))
    upstream = centred(arg_keys[1], (NODES, HID), 1.0, 6.0, ((0, 256),))
    tile_values = centred(arg_keys[2], (N_ROW, N_COL, TILES_DEV, TILE, TILE), (TILES_DEV * TILE * N_COL * 5 // (8 * ROW_TILES)) ** -0.5, 0.046875, ((0, 32), (1, 8)))
    tile_rows = draw_tile_rows(jax.random.fold_in(arg_keys[10], 71), 0)
    tile_cols = draw_tile_cols(jax.random.fold_in(arg_keys[10], 71), 0)
    tile_count = draw_tile_count(jax.random.fold_in(arg_keys[10], 71), 0)
    w_one = centred(arg_keys[6], (F, HID), F ** -0.5, 0.5)
    b_one = centred(arg_keys[7], (HID,), 0.5, 3.0, (), jnp.float32)
    w_two = centred(arg_keys[8], (HID, HID), HID ** -0.5, 0.375)
    b_two = centred(arg_keys[9], (HID,), 0.5, 3.0, (), jnp.float32)
    return dict(features=features, upstream=upstream, tile_values=tile_values, tile_rows=tile_rows, tile_cols=tile_cols, tile_count=tile_count, w_one=w_one, b_one=b_one, w_two=w_two, b_two=b_two)


def dsilu(value):
    sig = jax.nn.sigmoid(value)
    return sig * (1.0 + value * (1.0 - sig))


def local_forward(values, rows, cols, count, source, row_tiles):
    tile = values.shape[-1]
    width = source.shape[1]
    picked = source.reshape(-1, tile, width)[cols]
    product = jnp.einsum("tab,tbf->taf", values.astype(jnp.float32), picked.astype(jnp.float32))
    live = jnp.arange(values.shape[0], dtype=jnp.int32) < count
    onehot = ((rows[:, None] == jnp.arange(row_tiles, dtype=jnp.int32)[None, :]) & live[:, None]).astype(jnp.float32)
    return jnp.einsum("tr,taf->raf", onehot, product).reshape(row_tiles * tile, width)


def local_backward(values, rows, cols, count, source, col_tiles):
    tile = values.shape[-1]
    width = source.shape[1]
    picked = source.reshape(-1, tile, width)[rows]
    product = jnp.einsum("tab,taf->tbf", values.astype(jnp.float32), picked.astype(jnp.float32))
    live = jnp.arange(values.shape[0], dtype=jnp.int32) < count
    onehot = ((cols[:, None] == jnp.arange(col_tiles, dtype=jnp.int32)[None, :]) & live[:, None]).astype(jnp.float32)
    return jnp.einsum("tc,taf->caf", onehot, product).reshape(col_tiles * tile, width)


def reference(features, upstream, tile_values, tile_rows, tile_cols, tile_count, w_one, b_one, w_two, b_two):
    def aggregate(source):
        width = source.shape[1]
        blocks = source.reshape(N_COL, N_ROW * ROWS_DEV, width)

        def per_row(i):
            def step(total, j):
                part = local_forward(tile_values[i, j], tile_rows[i, j], tile_cols[i, j], tile_count[i, j], blocks[j], ROW_TILES)
                return total + part, None

            total, _ = lax.scan(step, jnp.zeros((N_COL * ROWS_DEV, width), jnp.float32), jnp.arange(N_COL, dtype=jnp.int32))
            return total

        result = lax.map(per_row, jnp.arange(N_ROW, dtype=jnp.int32))
        return result.reshape(N_ROW, N_COL, ROWS_DEV, width).transpose(1, 0, 2, 3).reshape(NODES, width)

    def transposed(source):
        width = source.shape[1]
        blocks = source.reshape(N_COL, N_ROW, ROWS_DEV, width)

        def per_col(j):
            def step(total, i):
                rows_here = blocks[:, i].reshape(N_COL * ROWS_DEV, width)
                part = local_backward(tile_values[i, j], tile_rows[i, j], tile_cols[i, j], tile_count[i, j], rows_here, COL_TILES)
                return total + part, None

            total, _ = lax.scan(step, jnp.zeros((N_ROW * ROWS_DEV, width), jnp.float32), jnp.arange(N_ROW, dtype=jnp.int32))
            return total

        return lax.map(per_col, jnp.arange(N_COL, dtype=jnp.int32)).reshape(NODES, width)

    agg_in = aggregate(features).astype(jnp.bfloat16)
    pre_one = jnp.dot(agg_in, w_one, preferred_element_type=jnp.float32) + b_one
    hidden_one = jax.nn.silu(pre_one).astype(jnp.bfloat16)
    agg_hidden = aggregate(hidden_one).astype(jnp.bfloat16)
    pre_two = jnp.dot(agg_hidden, w_two, preferred_element_type=jnp.float32) + b_two
    hidden_out = jax.nn.silu(pre_two).astype(jnp.bfloat16)
    grad_two = (upstream.astype(jnp.float32) * dsilu(pre_two)).astype(jnp.bfloat16)
    grad_w_two = jnp.dot(agg_hidden.T, grad_two, preferred_element_type=jnp.float32)
    grad_b_two = jnp.sum(grad_two.astype(jnp.float32), axis=0)
    back_two = jnp.dot(grad_two, w_two.T, preferred_element_type=jnp.float32).astype(jnp.bfloat16)
    back_agg = transposed(back_two)
    grad_one = (back_agg * dsilu(pre_one)).astype(jnp.bfloat16)
    grad_w_one = jnp.dot(agg_in.T, grad_one, preferred_element_type=jnp.float32)
    grad_b_one = jnp.sum(grad_one.astype(jnp.float32), axis=0)
    return (hidden_out, grad_w_one, grad_b_one, grad_w_two, grad_b_two)
```

```python
import functools

import jax
import jax.numpy as jnp
from jax import lax
from jax.experimental import pallas as pl
from jax.experimental.pallas import tpu as pltpu
from jax.sharding import PartitionSpec as P

MESH = pl.DeviceIdType.MESH
BF = jnp.bfloat16
F32 = jnp.float32


def dsilu_from(value, sig):
    return sig * (1.0 + value * (1.0 - sig))


def matmul(left, right):
    return jnp.dot(left, right, preferred_element_type=F32)


def wait_for(ref, sem):
    pltpu.make_async_copy(ref, ref, sem).wait()


def send(src, dst, send_sem, recv_sem, **where):
    pltpu.make_async_remote_copy(
        src_ref=src,
        dst_ref=dst,
        send_sem=send_sem,
        recv_sem=recv_sem,
        device_id=where,
        device_id_type=MESH,
    ).start()


def kernel(
    nz, nx, ncol,
    slot_of, features, upstream, tiles_hbm, w_one, b_one, w_two, b_two,
    hidden_out, grad_w_one, grad_b_one, grad_w_two, grad_b_two,
    tiles, dense, dense_t, gath_x, gath_a, agg_t, slope, hid, acc_one, acc_two,
    part_one, land_one, part_two, land_two, back,
    gone, piece_one, land_p1, col_p1, full_p1, piece_two, land_p2, col_p2, full_p2,
    bias_c, bias_x, bias_z, acc_w, acc_b, agg_h, agg_ht, grad_h, local_two,
    tile_sem, ssem, recv_x, recv_a, recv_c, recv_back, recv_w,
):
    nrow = nz * nx
    slots = tiles.shape[0] - 1
    width = features.shape[1]
    hidden = w_one.shape[1]
    half = gath_x.shape[2]
    row = lax.axis_index("row")
    col = lax.axis_index("col")
    mz = row // nx
    mx = lax.rem(row, nx)
    parity = lax.rem(col, 2)

    tile_copy = pltpu.make_async_copy(tiles_hbm.at[0, 0], tiles.at[pl.ds(0, slots)], tile_sem)
    tile_copy.start()
    tiles[slots] = jnp.zeros(tiles.shape[1:], BF)

    barrier = pltpu.get_barrier_semaphore()

    @pl.loop(1, nrow)
    def _(d):
        pl.semaphore_signal(
            barrier, inc=1, device_id={"row": lax.rem(row + d, nrow)}, device_id_type=MESH
        )

    @pl.loop(1, ncol)
    def _(d):
        pl.semaphore_signal(
            barrier, inc=1, device_id={"col": lax.rem(col + d, ncol)}, device_id_type=MESH
        )

    def gather_row(buf, rsem, ssem_, compute, between):
        def push(h, first, count, where):
            part = buf.at[h, pl.ds(first, count)]
            send(part, part, ssem_, rsem.at[h, first], row=where)

        def arrived(h, first, count):
            wait_for(buf.at[h, pl.ds(first, count)], rsem.at[h, first])

        def peer(d):
            return mz * nx + lax.rem(mx + d, nx)

        up = lax.rem(mz + 1, nz) * nx + mx
        down = lax.rem(mz + nz - 1, nz) * nx + mx
        last = nz // 2
        for d in range(1, nx):
            push(1, row, 1, peer(d))

        def onward(h, width_, lower, upper, step):
            if step < last:
                push(h, lower, width_, up)
                push(h, upper, width_, down)
            else:
                push(
                    h,
                    jnp.where(parity == 0, lower, upper),
                    width_,
                    jnp.where(parity == 0, up, down),
                )

        onward(0, 1, row, row, 1)
        for d in range(1, nx):
            push(0, row, 1, peer(d))
        for d in range(1, nx):
            arrived(1, peer(d), 1)
        onward(1, nx, mz * nx, mz * nx, 1)
        ready = [mz]
        for s in range(1, last + 1):
            lower = lax.rem(mz + nz - s, nz)
            upper = lax.rem(mz + s, nz)
            now = [lower, upper] if s < last else [upper]
            for zp in now:
                arrived(0, zp * nx + mx, 1)
            if s < last:
                onward(0, 1, lower * nx + mx, upper * nx + mx, s + 1)
            for zp in now:
                for d in range(1, nx):
                    push(0, zp * nx + mx, 1, peer(d))
            for zp in now:
                arrived(1, zp * nx, nx)
            if s < last:
                onward(1, nx, lower * nx, upper * nx, s + 1)
            if s == 1:
                between()
            for zp in ready:
                for d in range(1, nx):
                    arrived(0, zp * nx + lax.rem(mx + d, nx), 1)
                compute(zp)
            ready = now
        for zp in ready:
            for d in range(1, nx):
                arrived(0, zp * nx + lax.rem(mx + d, nx), 1)
            compute(zp)

    def scatter_col(acc, part, land, rsem, ssem_):
        @pl.loop(1, ncol)
        def _(d):
            to = lax.rem(col + d, ncol)
            part[to] = acc[to].astype(BF)
            send(part.at[to], land.at[col], ssem_, rsem, col=to)

    def scattered_col(acc, land, rsem):
        wait_for(land.at[pl.ds(0, ncol - 1)], rsem)
        total = acc[col]
        for d in range(1, ncol):
            total = total + land[lax.rem(col + d, ncol)].astype(F32)
        return total.astype(BF)

    def build_dense():
        tile_copy.wait()

        @pl.loop(0, nz)
        def _(zp):
            for r in range(ncol):
                for x in range(nx):
                    slot = slot_of[r * nrow + zp * nx + x]
                    dense[zp, pl.ds(r * 128, 128), pl.ds(x * 128, 128)] = tiles[slot]

    rows_step = min(256, ncol * 128)

    def layer_one(zp):
        source = jnp.concatenate(
            [gath_x[h, zp * nx + x] for x in range(nx) for h in range(2)], axis=0
        )

        @pl.loop(0, ncol * 128 // rows_step)
        def _(m):
            at = pl.ds(pl.multiple_of(m * rows_step, rows_step), rows_step)
            more = matmul(dense[zp, at], source).reshape(rows_step // 128, 128, width)
            tiles_at = pl.ds(m * (rows_step // 128), rows_step // 128)
            acc_one[tiles_at] = acc_one[tiles_at] + more

    def layer_two(zp):
        @pl.loop(0, nx)
        def _(x):
            source = jnp.concatenate([gath_a[h, zp * nx + x] for h in range(2)], axis=0)
            pre = matmul(source, w_one[...]) + b_one[...]
            sig = jax.nn.sigmoid(pre)
            at = pl.ds(pl.multiple_of(x * 128, 128), 128)
            slope[zp, at] = dsilu_from(pre, sig)
            hid[at] = (pre * sig).astype(BF)

        @pl.loop(0, ncol * 128 // rows_step)
        def _(m):
            at = pl.ds(pl.multiple_of(m * rows_step, rows_step), rows_step)
            more = matmul(dense[zp, at], hid[...]).reshape(rows_step // 128, 128, hidden)
            tiles_at = pl.ds(m * (rows_step // 128), rows_step // 128)
            acc_two[tiles_at] = acc_two[tiles_at] + more

    def set_own(buf, value):
        buf[0, row] = value[:half]
        buf[1, row] = value[half:]

    set_own(gath_x, features[...])
    acc_one[...] = jnp.zeros(acc_one.shape, F32)
    acc_two[...] = jnp.zeros(acc_two.shape, F32)
    pl.semaphore_wait(barrier, nrow - 1 + ncol - 1)

    gather_row(gath_x, recv_x, ssem.at[0], layer_one, build_dense)

    scatter_col(acc_one, part_one, land_one, recv_c.at[0], ssem.at[1])

    @pl.loop(0, nz)
    def _(zp):
        for r in range(ncol):
            for x in range(nx):
                dense_t[zp, pl.ds(x * 128, 128), pl.ds(r * 128, 128)] = dense[
                    zp, pl.ds(r * 128, 128), pl.ds(x * 128, 128)
                ].T

    set_own(gath_a, scattered_col(acc_one, land_one, recv_c.at[0]))
    gather_row(gath_a, recv_a, ssem.at[2], layer_two, lambda: None)

    scatter_col(acc_two, part_two, land_two, recv_c.at[1], ssem.at[3])

    @pl.loop(0, nz)
    def _(zp):
        for x in range(nx):
            source = jnp.concatenate([gath_a[h, zp * nx + x] for h in range(2)], axis=0)
            agg_t[zp, :, pl.ds(x * 128, 128)] = source.T

    agg_h[...] = scattered_col(acc_two, land_two, recv_c.at[1])

    @pl.loop(0, 2)
    def _(m):
        at = pl.ds(pl.multiple_of(m * 64, 64), 64)
        pre = matmul(agg_h[at], w_two[...]) + b_two[...]
        sig = jax.nn.sigmoid(pre)
        hidden_out[at] = (pre * sig).astype(BF)
        grad = (upstream[at].astype(F32) * dsilu_from(pre, sig)).astype(BF)
        grad_h[at] = grad
        back[pl.ds(pl.multiple_of(col * 128 + m * 64, 64), 64)] = lax.dot_general(
            grad, w_two[...], (((1,), (1,)), ((), ())), preferred_element_type=F32
        ).astype(BF)

    own_back = back.at[pl.ds(pl.multiple_of(col * 128, 128), 128)]

    @pl.loop(1, ncol)
    def _(d):
        send(own_back, own_back, ssem.at[4], recv_back, col=lax.rem(col + d, ncol))

    for m in range(hidden // 128):
        agg_ht[m] = agg_h[:, m * 128 : m * 128 + 128].T

    @pl.loop(0, hidden // 128)
    def _(m):
        local_two[m] = matmul(agg_ht[m], grad_h[...])

    local_w_two = local_two[...].reshape(hidden, hidden)
    local_b_two = jnp.sum(grad_h[...].astype(F32), axis=0, keepdims=True)

    def split_pieces(piece, value):
        per = piece.shape[1] // 8
        for t in range(nrow * per):
            r, c = t // (hidden // 128), t % (hidden // 128)
            piece[t // per, pl.ds((t % per) * 8, 8)] = value[
                r * 8 : r * 8 + 8, c * 128 : c * 128 + 128
            ]

    def join_pieces(piece, out):
        per = piece.shape[1] // 8
        for t in range(nrow * per):
            r, c = t // (hidden // 128), t % (hidden // 128)
            out[pl.ds(r * 8, 8), pl.ds(c * 128, 128)] = piece[t // per, pl.ds((t % per) * 8, 8)]

    def spread_row(piece, land, send_sem, recv_sem):
        @pl.loop(1, nrow)
        def _(d):
            to = lax.rem(row + d, nrow)
            send(piece.at[to], land.at[row], send_sem, recv_sem, row=to)

        land[row] = piece[row]

    def spread_same(buf, send_sem, recv_sem, size, me, axis):
        @pl.loop(1, size)
        def _(d):
            to = lax.rem(me + d, size)
            send(buf.at[me], buf.at[me], send_sem, recv_sem, **{axis: to})

    def total(buf):
        value = buf[0]
        for k in range(1, buf.shape[0]):
            value = value + buf[k]
        return value

    def all_but_one(buf):
        return buf.at[pl.ds(0, buf.shape[0] - 1)]

    split_pieces(piece_two, local_w_two)
    spread_row(piece_two, land_p2, ssem.at[5], recv_w.at[0])
    wait_for(all_but_one(land_p2), recv_w.at[0])
    col_p2[col] = total(land_p2)
    spread_same(col_p2, ssem.at[6], recv_w.at[1], ncol, col, "col")

    wait_for(back.at[pl.ds(0, (ncol - 1) * 128)], recv_back)

    def backward(first, last):
        @pl.loop(first, last)
        def _(zp):
            for p in range(nx * 128 // 256):
                at = pl.ds(p * 256, 256)
                grad_one = (matmul(dense_t[zp, at], back[...]) * slope[zp, at]).astype(BF)
                gone[at] = grad_one
                acc_b[...] = acc_b[...] + jnp.sum(
                    grad_one.astype(F32).reshape(32, 8, hidden), axis=0
                )
            acc_w[...] = acc_w[...] + matmul(agg_t[zp], gone[...])

    acc_w[...] = jnp.zeros(acc_w.shape, F32)
    acc_b[...] = jnp.zeros(acc_b.shape, F32)
    backward(0, nz // 2)
    wait_for(all_but_one(col_p2), recv_w.at[1])
    full_p2[row] = total(col_p2)
    spread_same(full_p2, ssem.at[7], recv_w.at[2], nrow, row, "row")
    backward(nz // 2, nz)

    split_pieces(piece_one, acc_w)
    spread_row(piece_one, land_p1, ssem.at[8], recv_w.at[3])
    local_b_one = jnp.sum(acc_b[...], axis=0, keepdims=True)
    for k, value in enumerate((local_b_one, local_b_two)):
        for c in range(hidden // 128):
            bias_c[col, pl.ds(k * (hidden // 128) + c, 1)] = value[:, c * 128 : c * 128 + 128]
    spread_same(bias_c, ssem.at[9], recv_w.at[4], ncol, col, "col")
    wait_for(all_but_one(land_p1), recv_w.at[3])
    col_p1[col] = total(land_p1)
    spread_same(col_p1, ssem.at[10], recv_w.at[5], ncol, col, "col")
    wait_for(all_but_one(bias_c), recv_w.at[4])
    bias_x[mx] = total(bias_c)

    @pl.loop(1, nx)
    def _(d):
        send(
            bias_x.at[mx], bias_x.at[mx], ssem.at[11], recv_w.at[6],
            row=mz * nx + lax.rem(mx + d, nx),
        )

    wait_for(all_but_one(col_p1), recv_w.at[5])
    full_p1[row] = total(col_p1)
    spread_same(full_p1, ssem.at[12], recv_w.at[7], nrow, row, "row")
    wait_for(all_but_one(bias_x), recv_w.at[6])
    bias_z[mz] = total(bias_x)

    @pl.loop(1, nz)
    def _(d):
        send(
            bias_z.at[mz], bias_z.at[mz], ssem.at[13], recv_w.at[8],
            row=lax.rem(mz + d, nz) * nx + mx,
        )

    wait_for(all_but_one(full_p2), recv_w.at[2])
    join_pieces(full_p2, grad_w_two)
    wait_for(all_but_one(bias_z), recv_w.at[8])
    biases = total(bias_z)
    for k, out in enumerate((grad_b_one, grad_b_two)):
        for c in range(hidden // 128):
            at = k * (hidden // 128) + c
            out[:, pl.ds(c * 128, 128)] = biases[at : at + 1]
    wait_for(all_but_one(full_p1), recv_w.at[7])
    join_pieces(full_p1, grad_w_one)

    wait_for(gath_x.at[:, pl.ds(0, nrow - 1)], ssem.at[0])
    wait_for(all_but_one(part_one), ssem.at[1])
    wait_for(gath_a.at[:, pl.ds(0, nrow - 1)], ssem.at[2])
    wait_for(all_but_one(part_two), ssem.at[3])
    wait_for(back.at[pl.ds(0, (ncol - 1) * 128)], ssem.at[4])
    for k, buf in enumerate(
        (land_p2, col_p2, full_p2, land_p1, bias_c, col_p1, bias_x, full_p1, bias_z)
    ):
        wait_for(all_but_one(buf), ssem.at[5 + k])


def per_device(
    mesh_shape,
    features, upstream, tile_values, tile_rows, tile_cols, tile_count, w_one, b_one, w_two, b_two,
):
    nz, nx, ncol = mesh_shape
    nrow = nz * nx
    slots = tile_values.shape[2]
    width = features.shape[1]
    hidden = w_one.shape[1]
    index = jnp.arange(slots, dtype=jnp.int32)
    place = jnp.where(index < tile_count[0, 0], tile_rows[0, 0] * nrow + tile_cols[0, 0], -1)
    hit = place[None, :] == jnp.arange(ncol * nrow, dtype=jnp.int32)[:, None]
    slot_of = slots + jnp.sum(jnp.where(hit, index[None, :] - slots, 0), axis=1)

    vmem = pl.BlockSpec(memory_space=pltpu.VMEM)
    per_one = width * hidden // (8 * 128) // nrow * 8
    per_two = hidden * hidden // (8 * 128) // nrow * 8
    scratch = [
        pltpu.VMEM((slots + 1, 128, 128), BF),
        pltpu.VMEM((nz, ncol * 128, nx * 128), BF),
        pltpu.VMEM((nz, nx * 128, ncol * 128), BF),
        pltpu.VMEM((2, nrow, 64, width), BF),
        pltpu.VMEM((2, nrow, 64, width), BF),
        pltpu.VMEM((nz, width, nx * 128), BF),
        pltpu.VMEM((nz, nx * 128, hidden), F32),
        pltpu.VMEM((nx * 128, hidden), BF),
        pltpu.VMEM((ncol, 128, width), F32),
        pltpu.VMEM((ncol, 128, hidden), F32),
        pltpu.VMEM((ncol, 128, width), BF),
        pltpu.VMEM((ncol, 128, width), BF),
        pltpu.VMEM((ncol, 128, hidden), BF),
        pltpu.VMEM((ncol, 128, hidden), BF),
        pltpu.VMEM((ncol * 128, hidden), BF),
        pltpu.VMEM((nx * 128, hidden), BF),
        pltpu.VMEM((nrow, per_one, 128), F32),
        pltpu.VMEM((nrow, per_one, 128), F32),
        pltpu.VMEM((ncol, per_one, 128), F32),
        pltpu.VMEM((nrow, per_one, 128), F32),
        pltpu.VMEM((nrow, per_two, 128), F32),
        pltpu.VMEM((nrow, per_two, 128), F32),
        pltpu.VMEM((ncol, per_two, 128), F32),
        pltpu.VMEM((nrow, per_two, 128), F32),
        pltpu.VMEM((ncol, 8, 128), F32),
        pltpu.VMEM((nx, 8, 128), F32),
        pltpu.VMEM((nz, 8, 128), F32),
        pltpu.VMEM((width, hidden), F32),
        pltpu.VMEM((8, hidden), F32),
        pltpu.VMEM((128, hidden), BF),
        pltpu.VMEM((hidden // 128, 128, 128), BF),
        pltpu.VMEM((128, hidden), BF),
        pltpu.VMEM((hidden // 128, 128, hidden), F32),
        pltpu.SemaphoreType.DMA,
        pltpu.SemaphoreType.DMA((14,)),
        pltpu.SemaphoreType.DMA((2, nrow)),
        pltpu.SemaphoreType.DMA((2, nrow)),
        pltpu.SemaphoreType.DMA((2,)),
        pltpu.SemaphoreType.DMA,
        pltpu.SemaphoreType.DMA((9,)),
    ]
    out = pl.pallas_call(
        functools.partial(kernel, nz, nx, ncol),
        out_shape=(
            jax.ShapeDtypeStruct((128, hidden), BF),
            jax.ShapeDtypeStruct((width, hidden), F32),
            jax.ShapeDtypeStruct((1, hidden), F32),
            jax.ShapeDtypeStruct((hidden, hidden), F32),
            jax.ShapeDtypeStruct((1, hidden), F32),
        ),
        in_specs=[
            pl.BlockSpec(memory_space=pltpu.SMEM), vmem, vmem,
            pl.BlockSpec(memory_space=pl.ANY), vmem, vmem, vmem, vmem,
        ],
        out_specs=(vmem,) * 5,
        scratch_shapes=scratch,
        compiler_params=pltpu.CompilerParams(
            collective_id=0, has_side_effects=True, vmem_limit_bytes=56 * 1024 * 1024
        ),
    )(
        slot_of, features, upstream, tile_values, w_one, b_one.reshape(1, hidden),
        w_two, b_two.reshape(1, hidden),
    )
    hidden_out, grad_w_one, grad_b_one, grad_w_two, grad_b_two = out
    return (
        hidden_out, grad_w_one, grad_b_one.reshape(hidden), grad_w_two, grad_b_two.reshape(hidden)
    )


def solution(mesh, nx=4):
    nrow, ncol = mesh.shape["row"], mesh.shape["col"]
    in_specs = (
        P(("col", "row"), None),
        P(("col", "row"), None),
        P("row", "col", None, None, None),
        P("row", "col", None),
        P("row", "col", None),
        P("row", "col"),
        P(),
        P(),
        P(),
        P(),
    )
    out_specs = (P(("col", "row"), None), P(), P(), P(), P())
    return jax.shard_map(
        functools.partial(per_device, (nrow // nx, nx, ncol)),
        mesh=mesh, in_specs=in_specs, out_specs=out_specs, check_vma=False,
    )
```

```python
import functools

import jax
import jax.numpy as jnp
from jax import lax
from jax.experimental import pallas as pl
from jax.experimental.pallas import tpu as pltpu
from jax.sharding import PartitionSpec as P

MESH = pl.DeviceIdType.MESH
BF = jnp.bfloat16
F32 = jnp.float32


def dsilu_from(value, sig):
    return sig * (1.0 + value * (1.0 - sig))


def matmul(left, right):
    return jnp.dot(left, right, preferred_element_type=F32)


def wait_for(ref, sem):
    pltpu.make_async_copy(ref, ref, sem).wait()


def send(src, dst, send_sem, recv_sem, **where):
    pltpu.make_async_remote_copy(
        src_ref=src,
        dst_ref=dst,
        send_sem=send_sem,
        recv_sem=recv_sem,
        device_id=where,
        device_id_type=MESH,
    ).start()


def kernel(
    nz, nx, ncol,
    count, features, upstream_hbm, tiles_hbm, rows_hbm, cols_hbm,
    w_one_hbm, b_one_hbm, w_two_hbm, b_two_hbm,
    hidden_out, grad_w_one, grad_b_one, grad_w_two, grad_b_two,
    tiles, dense, dense_t, gz_x, gx_x, gz_a, gx_a, agg_t, slope, hid, acc_one, acc_two,
    part_one, land_one, part_two, land_two, back,
    gone, piece_one, land_p1, z_p1, full_p1, piece_two, land_p2, z_p2, full_p2,
    bias_c, bias_x, bias_z, acc_w, acc_b, agg_h, agg_ht, grad_h, local_two,
    upstream, w_one, b_one, w_two, b_two, rows_of, cols_of, slots_vmem, slot_of,
    tile_sem, in_sem, ssem, recv_x, recv_a, recv_c, recv_back, recv_w,
):
    nrow = nz * nx
    slots = tiles.shape[0] - 1
    width = features.shape[1]
    hidden = w_one.shape[1]
    far_first = [nz // 2] + [d * g for d in range(nz // 2 - 1, 0, -1) for g in (1, -1)]
    row = lax.axis_index("row")
    col = lax.axis_index("col")
    mz = row // nx
    mx = lax.rem(row, nx)
    group = mx * ncol + col
    ngroup = nx * ncol
    cut = gz_x.shape[1]

    tile_copy = pltpu.make_async_copy(tiles_hbm.at[0, 0], tiles.at[pl.ds(0, slots)], tile_sem)
    own_copies = [
        pltpu.make_async_copy(src, dst, in_sem.at[k])
        for k, (src, dst) in enumerate((
            (rows_hbm.at[0], rows_of),
            (cols_hbm.at[0], cols_of),
            (features.at[pl.ds(0, cut)], gz_x.at[row]),
            (features.at[pl.ds(cut, 128 - cut)], gx_x.at[row]),
            (w_one_hbm, w_one),
            (b_one_hbm, b_one),
            (w_two_hbm, w_two),
            (b_two_hbm, b_two),
            (upstream_hbm, upstream),
        ))
    ]
    for copy in own_copies:
        copy.start()
    tile_copy.start()

    barrier = pltpu.get_barrier_semaphore()

    def member(d):
        to = lax.rem(group + d, ngroup)
        return to, {"row": mz * nx + to // ncol, "col": lax.rem(to, ncol)}

    @pl.loop(1, nz)
    def _(d):
        pl.semaphore_signal(
            barrier, inc=1, device_id={"row": lax.rem(mz + d, nz) * nx + mx}, device_id_type=MESH
        )

    @pl.loop(1, ngroup)
    def _(d):
        pl.semaphore_signal(barrier, inc=1, device_id=member(d)[1], device_id_type=MESH)

    def peer_x(d):
        return lax.rem(mx + d, nx)

    def peer_z(d):
        return lax.rem(mz + d + nz, nz)

    def gather_row(by_z, by_x, own_z, own_x, rsem, ssem_, compute, placed, between):
        def push(buf, sems, first, number, z, x):
            part = buf.at[pl.ds(first, number)]
            send(part, part, ssem_, sems.at[first], row=z * nx + x)

        def push_own(buf, own, sems, z, x):
            send(own, buf.at[row], ssem_, sems.at[row], row=z * nx + x)

        def arrived(buf, sems, first, number):
            wait_for(buf.at[pl.ds(first, number)], sems.at[first])

        sems_z, sems_x = rsem.at[0], rsem.at[1]
        for d in range(1, nx):
            push_own(by_x, own_x, sems_x, mz, peer_x(d))
        for d in far_first[::-1]:
            push_own(by_z, own_z, sems_z, peer_z(d), mx)
        for d in range(1, nx):
            push_own(by_z, own_z, sems_z, mz, peer_x(d))
        placed()
        for d in range(1, nx):
            arrived(by_x, sems_x, mz * nx + peer_x(d), 1)
        for d in far_first[::-1]:
            push(by_x, sems_x, mz * nx, nx, peer_z(d), mx)

        def onward(d):
            at = peer_z(d) * nx + mx
            arrived(by_z, sems_z, at, 1)
            for e in range(1, nx):
                push(by_z, sems_z, at, 1, mz, peer_x(e))

        def use(d):
            for e in range(1, nx):
                arrived(by_z, sems_z, peer_z(d) * nx + peer_x(e), 1)
            if d:
                arrived(by_x, sems_x, peer_z(d) * nx, nx)
            compute(peer_z(d))

        between()
        near_first = far_first[::-1]
        early = len(near_first) // 2 + 1
        for d in near_first[:early]:
            onward(d)
        use(0)
        for d in near_first[early:]:
            onward(d)
        for d in near_first:
            use(d)

    def scatter_col(acc, part, land, rsem, ssem_):
        @pl.loop(1, ncol)
        def _(d):
            to = lax.rem(col + d, ncol)
            part[to] = acc[to].astype(BF)
            send(part.at[to], land.at[col], ssem_, rsem, col=to)

    def scattered_col(acc, land, rsem):
        wait_for(land.at[pl.ds(0, ncol - 1)], rsem)
        total = acc[col]
        for d in range(1, ncol):
            total = total + land[lax.rem(col + d, ncol)].astype(F32)
        return total.astype(BF)

    def own_placed():
        own_copies[2].wait()
        own_copies[3].wait()

    def find_slots():
        own_copies[0].wait()
        own_copies[1].wait()
        places = ncol * nrow
        index = lax.broadcasted_iota(jnp.int32, (1, slots), 1)
        place = jnp.where(index < count[0, 0], rows_of[...] * nrow + cols_of[...], -1)
        column = jnp.broadcast_to(place, (8, slots)).T[:, :1]
        hit = column == lax.broadcasted_iota(jnp.int32, (slots, places), 1)
        entry = lax.broadcasted_iota(jnp.int32, (slots, places), 0) - slots
        found = jnp.sum(jnp.where(hit, entry, 0), axis=0, keepdims=True) + slots
        slots_vmem[...] = jnp.broadcast_to(found, slots_vmem.shape)
        to_smem = pltpu.make_async_copy(slots_vmem, slot_of, in_sem.at[0])
        to_smem.start()
        tiles[slots] = jnp.zeros(tiles.shape[1:], BF)
        acc_one[...] = jnp.zeros(acc_one.shape, F32)
        acc_two[...] = jnp.zeros(acc_two.shape, F32)
        for copy in own_copies[4:]:
            copy.wait()
        to_smem.wait()
        tile_copy.wait()

    def build_dense(zp):
        for r in range(ncol):
            for x in range(nx):
                slot = jnp.clip(slot_of[0, r * nrow + zp * nx + x], 0, slots)
                dense[zp, pl.ds(r * 128, 128), pl.ds(x * 128, 128)] = tiles[slot]

    rows_step = min(1024, ncol * 128)

    def layer_one(zp):
        build_dense(zp)
        source = jnp.concatenate(
            [buf[zp * nx + x] for x in range(nx) for buf in (gz_x, gx_x)], axis=0
        )

        @pl.loop(0, ncol * 128 // rows_step)
        def _(m):
            at = pl.ds(pl.multiple_of(m * rows_step, rows_step), rows_step)
            more = matmul(dense[zp, at], source).reshape(rows_step // 128, 128, width)
            tiles_at = pl.ds(m * (rows_step // 128), rows_step // 128)
            acc_one[tiles_at] = acc_one[tiles_at] + more

    def layer_two(zp):
        for x in range(nx):
            source = jnp.concatenate([gz_a[zp * nx + x], gx_a[zp * nx + x]], axis=0)
            pre = matmul(source, w_one[...]) + b_one[...]
            sig = jax.nn.sigmoid(pre)
            at = pl.ds(x * 128, 128)
            slope[zp, at] = dsilu_from(pre, sig)
            hid[at] = (pre * sig).astype(BF)

        @pl.loop(0, ncol * 128 // rows_step)
        def _(m):
            at = pl.ds(pl.multiple_of(m * rows_step, rows_step), rows_step)
            more = matmul(dense[zp, at], hid[...]).reshape(rows_step // 128, 128, hidden)
            tiles_at = pl.ds(m * (rows_step // 128), rows_step // 128)
            acc_two[tiles_at] = acc_two[tiles_at] + more

    def set_own(by_z, by_x, value):
        by_z[row] = value[:cut]
        by_x[row] = value[cut:]

    pl.semaphore_wait(barrier, nz - 1 + ngroup - 1)

    gather_row(
        gz_x, gx_x, features.at[pl.ds(0, cut)], features.at[pl.ds(cut, 128 - cut)],
        recv_x, ssem.at[0], layer_one, own_placed, find_slots,
    )


    scatter_col(acc_one, part_one, land_one, recv_c.at[0], ssem.at[1])

    @pl.loop(0, nz)
    def _(zp):
        for r in range(ncol):
            for x in range(nx):
                dense_t[zp, pl.ds(x * 128, 128), pl.ds(r * 128, 128)] = dense[
                    zp, pl.ds(r * 128, 128), pl.ds(x * 128, 128)
                ].T

    set_own(gz_a, gx_a, scattered_col(acc_one, land_one, recv_c.at[0]))

    gather_row(
        gz_a, gx_a, gz_a.at[row], gx_a.at[row], recv_a, ssem.at[2], layer_two,
        lambda: None, lambda: None,
    )


    scatter_col(acc_two, part_two, land_two, recv_c.at[1], ssem.at[3])

    @pl.loop(0, nz)
    def _(zp):
        for x in range(nx):
            source = jnp.concatenate([gz_a[zp * nx + x], gx_a[zp * nx + x]], axis=0)
            agg_t[zp, :, pl.ds(x * 128, 128)] = source.T

    agg_h[...] = scattered_col(acc_two, land_two, recv_c.at[1])

    @pl.loop(0, 2)
    def _(m):
        at = pl.ds(pl.multiple_of(m * 64, 64), 64)
        pre = matmul(agg_h[at], w_two[...]) + b_two[...]
        sig = jax.nn.sigmoid(pre)
        hidden_out[at] = (pre * sig).astype(BF)
        grad = (upstream[at].astype(F32) * dsilu_from(pre, sig)).astype(BF)
        grad_h[at] = grad
        back[pl.ds(pl.multiple_of(col * 128 + m * 64, 64), 64)] = lax.dot_general(
            grad, w_two[...], (((1,), (1,)), ((), ())), preferred_element_type=F32
        ).astype(BF)

    own_back = back.at[pl.ds(pl.multiple_of(col * 128, 128), 128)]

    @pl.loop(1, ncol)
    def _(d):
        send(own_back, own_back, ssem.at[4], recv_back, col=lax.rem(col + d, ncol))

    for m in range(hidden // 128):
        agg_ht[m] = agg_h[:, m * 128 : m * 128 + 128].T

    @pl.loop(0, hidden // 128)
    def _(m):
        local_two[m] = matmul(agg_ht[m], grad_h[...])

    local_w_two = local_two[...].reshape(hidden, hidden)
    local_b_two = jnp.sum(grad_h[...].astype(F32), axis=0, keepdims=True)

    def tile_places(per):
        for t in range(ngroup * per // 8):
            r, c = t // (hidden // 128), t % (hidden // 128)
            yield t // (per // 8), pl.ds(t % (per // 8) * 8, 8), slice(r * 8, r * 8 + 8), slice(c * 128, c * 128 + 128)

    def split_pieces(piece, value):
        for n, at, r, c in tile_places(piece.shape[1]):
            piece[n, at] = value[r, c].astype(piece.dtype)

    def join_pieces(piece, out):
        for n, at, r, c in tile_places(piece.shape[1]):
            out[r, c] = piece[n, at]

    def spread_group(piece, land, send_sem, recv_sem):
        @pl.loop(1, ngroup)
        def _(d):
            to, where = member(d)
            send(piece.at[to], land.at[group], send_sem, recv_sem, **where)

        land[group] = piece[group]

    def gather_group(buf, send_sem, recv_sem):
        @pl.loop(1, ngroup)
        def _(d):
            send(buf.at[group], buf.at[group], send_sem, recv_sem, **member(d)[1])

    def share(buf, send_sem, recv_sem, me, where):
        @pl.loop(1, buf.shape[0])
        def _(d):
            send(
                buf.at[me], buf.at[me], send_sem, recv_sem,
                **where(lax.rem(me + d, buf.shape[0])),
            )

    def along_z(z):
        return {"row": z * nx + mx}

    def along_x(x):
        return {"row": mz * nx + x}

    def along_col(c):
        return {"col": c}

    def total(buf):
        value = buf[0].astype(F32)
        for k in range(1, buf.shape[0]):
            value = value + buf[k].astype(F32)
        return value

    def all_but_one(buf):
        return buf.at[pl.ds(0, buf.shape[0] - 1)]

    split_pieces(piece_two, local_w_two)
    spread_group(piece_two, land_p2, ssem.at[5], recv_w.at[0])

    wait_for(back.at[pl.ds(0, (ncol - 1) * 128)], recv_back)

    def backward(first, last):
        @pl.loop(first, last)
        def _(zp):
            for p in range(1):
                at = pl.ds(0, nx * 128)
                grad_one = (matmul(dense_t[zp, at], back[...]) * slope[zp, at]).astype(BF)
                gone[at] = grad_one
                acc_b[...] = acc_b[...] + jnp.sum(
                    grad_one.astype(F32).reshape(nx * 16, 8, hidden), axis=0
                )
            acc_w[...] = acc_w[...] + matmul(agg_t[zp], gone[...])

    acc_w[...] = jnp.zeros(acc_w.shape, F32)
    acc_b[...] = jnp.zeros(acc_b.shape, F32)
    backward(0, nz // 2)
    wait_for(all_but_one(land_p2), recv_w.at[0])
    z_p2[mz] = total(land_p2)
    share(z_p2, ssem.at[6], recv_w.at[1], mz, along_z)
    backward(nz // 2, nz)

    split_pieces(piece_one, acc_w)
    spread_group(piece_one, land_p1, ssem.at[7], recv_w.at[2])
    local_b_one = jnp.sum(acc_b[...], axis=0, keepdims=True)
    for k, value in enumerate((local_b_one, local_b_two)):
        for c in range(hidden // 128):
            bias_z[mz, pl.ds(k * (hidden // 128) + c, 1)] = value[:, c * 128 : c * 128 + 128]
    share(bias_z, ssem.at[8], recv_w.at[3], mz, along_z)
    wait_for(all_but_one(z_p2), recv_w.at[1])
    full_p2[group] = total(z_p2)
    gather_group(full_p2, ssem.at[9], recv_w.at[4])

    wait_for(all_but_one(land_p1), recv_w.at[2])
    z_p1[mz] = total(land_p1)
    share(z_p1, ssem.at[10], recv_w.at[5], mz, along_z)
    wait_for(all_but_one(bias_z), recv_w.at[3])
    bias_x[mx] = total(bias_z)
    share(bias_x, ssem.at[11], recv_w.at[6], mx, along_x)

    wait_for(all_but_one(full_p2), recv_w.at[4])
    join_pieces(full_p2, grad_w_two)

    wait_for(all_but_one(z_p1), recv_w.at[5])
    full_p1[group] = total(z_p1)
    gather_group(full_p1, ssem.at[12], recv_w.at[7])
    wait_for(all_but_one(bias_x), recv_w.at[6])
    bias_c[col] = total(bias_x)
    share(bias_c, ssem.at[13], recv_w.at[8], col, along_col)

    wait_for(all_but_one(bias_c), recv_w.at[8])
    biases = total(bias_c)
    for k, out in enumerate((grad_b_one, grad_b_two)):
        for c in range(hidden // 128):
            at = k * (hidden // 128) + c
            out[:, pl.ds(c * 128, 128)] = biases[at : at + 1]
    wait_for(all_but_one(full_p1), recv_w.at[7])
    join_pieces(full_p1, grad_w_one)

    for k, buf in ((0, gz_x), (2, gz_a)):
        wait_for(buf.at[pl.ds(0, nrow - 1)], ssem.at[k])
    for k, buf in ((0, gx_x), (2, gx_a)):
        wait_for(buf.at[pl.ds(0, nrow - 1)], ssem.at[k])
    wait_for(all_but_one(part_one), ssem.at[1])
    wait_for(all_but_one(part_two), ssem.at[3])
    wait_for(back.at[pl.ds(0, (ncol - 1) * 128)], ssem.at[4])
    for k, buf in enumerate(
        (piece_two, z_p2, piece_one, bias_z, full_p2, z_p1, bias_x, full_p1, bias_c)
    ):
        wait_for(all_but_one(buf), ssem.at[5 + k])


def hand_over(*refs):
    count = len(refs) // 2
    for src, dst in zip(refs[:count], refs[count:], strict=True):
        dst[...] = src[...]


def per_device(
    mesh_shape,
    features, upstream, tile_values, tile_rows, tile_cols, tile_count, w_one, b_one, w_two, b_two,
):
    nz, nx, ncol = mesh_shape
    nrow = nz * nx
    slots = tile_values.shape[2]
    width = features.shape[1]
    hidden = w_one.shape[1]
    ngroup = nx * ncol
    vmem = pl.BlockSpec(memory_space=pltpu.VMEM)
    anywhere = pl.BlockSpec(memory_space=pl.ANY)
    per_one = width * hidden // (8 * 128) // ngroup * 8
    per_two = hidden * hidden // (8 * 128) // ngroup * 8
    scratch = [
        pltpu.VMEM((slots + 1, 128, 128), BF),
        pltpu.VMEM((nz, ncol * 128, nx * 128), BF),
        pltpu.VMEM((nz, nx * 128, ncol * 128), BF),
        pltpu.VMEM((nrow, 96, width), BF),
        pltpu.VMEM((nrow, 32, width), BF),
        pltpu.VMEM((nrow, 96, width), BF),
        pltpu.VMEM((nrow, 32, width), BF),
        pltpu.VMEM((nz, width, nx * 128), BF),
        pltpu.VMEM((nz, nx * 128, hidden), F32),
        pltpu.VMEM((nx * 128, hidden), BF),
        pltpu.VMEM((ncol, 128, width), F32),
        pltpu.VMEM((ncol, 128, hidden), F32),
        pltpu.VMEM((ncol, 128, width), BF),
        pltpu.VMEM((ncol, 128, width), BF),
        pltpu.VMEM((ncol, 128, hidden), BF),
        pltpu.VMEM((ncol, 128, hidden), BF),
        pltpu.VMEM((ncol * 128, hidden), BF),
        pltpu.VMEM((nx * 128, hidden), BF),
        pltpu.VMEM((ngroup, per_one, 128), F32),
        pltpu.VMEM((ngroup, per_one, 128), F32),
        pltpu.VMEM((nz, per_one, 128), F32),
        pltpu.VMEM((ngroup, per_one, 128), F32),
        pltpu.VMEM((ngroup, per_two, 128), BF),
        pltpu.VMEM((ngroup, per_two, 128), BF),
        pltpu.VMEM((nz, per_two, 128), F32),
        pltpu.VMEM((ngroup, per_two, 128), F32),
        pltpu.VMEM((ncol, 8, 128), F32),
        pltpu.VMEM((nx, 8, 128), F32),
        pltpu.VMEM((nz, 8, 128), F32),
        pltpu.VMEM((width, hidden), F32),
        pltpu.VMEM((8, hidden), F32),
        pltpu.VMEM((128, hidden), BF),
        pltpu.VMEM((hidden // 128, 128, 128), BF),
        pltpu.VMEM((128, hidden), BF),
        pltpu.VMEM((hidden // 128, 128, hidden), F32),
        pltpu.VMEM((128, hidden), BF),
        pltpu.VMEM((width, hidden), BF),
        pltpu.VMEM((1, hidden), F32),
        pltpu.VMEM((hidden, hidden), BF),
        pltpu.VMEM((1, hidden), F32),
        pltpu.VMEM((1, slots), jnp.int32),
        pltpu.VMEM((1, slots), jnp.int32),
        pltpu.VMEM((8, ncol * nrow), jnp.int32),
        pltpu.SMEM((8, ncol * nrow), jnp.int32),
        pltpu.SemaphoreType.DMA,
        pltpu.SemaphoreType.DMA((9,)),
        pltpu.SemaphoreType.DMA((14,)),
        pltpu.SemaphoreType.DMA((2, nrow)),
        pltpu.SemaphoreType.DMA((2, nrow)),
        pltpu.SemaphoreType.DMA((2,)),
        pltpu.SemaphoreType.DMA,
        pltpu.SemaphoreType.DMA((9,)),
    ]
    out = pl.pallas_call(
        functools.partial(kernel, nz, nx, ncol),
        out_shape=(
            jax.ShapeDtypeStruct((128, hidden), BF),
            jax.ShapeDtypeStruct((width, hidden), F32),
            jax.ShapeDtypeStruct((1, hidden), F32),
            jax.ShapeDtypeStruct((hidden, hidden), F32),
            jax.ShapeDtypeStruct((1, hidden), F32),
        ),
        in_specs=[
            pl.BlockSpec(memory_space=pltpu.SMEM), *([anywhere] * 9),
        ],
        out_specs=(vmem,) * 5,
        scratch_shapes=scratch,
        compiler_params=pltpu.CompilerParams(
            collective_id=0, has_side_effects=True, vmem_limit_bytes=56 * 1024 * 1024
        ),
    )(
        tile_count, features, upstream, tile_values, tile_rows, tile_cols,
        w_one, b_one.reshape(1, hidden), w_two, b_two.reshape(1, hidden),
    )
    hidden_out, grad_w_one, grad_b_one, grad_w_two, grad_b_two = pl.pallas_call(
        hand_over,
        out_shape=tuple(jax.ShapeDtypeStruct(o.shape, o.dtype) for o in out),
        in_specs=[vmem] * 5,
        out_specs=(vmem,) * 5,
    )(*out)
    return (
        hidden_out, grad_w_one, grad_b_one.reshape(hidden), grad_w_two, grad_b_two.reshape(hidden)
    )


def solution(mesh, nx=4):
    nrow, ncol = mesh.shape["row"], mesh.shape["col"]
    in_specs = (
        P(("col", "row"), None),
        P(("col", "row"), None),
        P("row", "col", None, None, None),
        P("row", "col", None),
        P("row", "col", None),
        P("row", "col"),
        P(),
        P(),
        P(),
        P(),
    )
    out_specs = (P(("col", "row"), None), P(), P(), P(), P())
    return jax.shard_map(
        functools.partial(per_device, (nrow // nx, nx, ncol)),
        mesh=mesh, in_specs=in_specs, out_specs=out_specs, check_vma=False,
    )
```

```python
import functools

import jax
import jax.numpy as jnp
from jax import lax
from jax.experimental import pallas as pl
from jax.experimental.pallas import tpu as pltpu
from jax.sharding import PartitionSpec as P

MESH = pl.DeviceIdType.MESH
BF = jnp.bfloat16
F32 = jnp.float32


def dsilu_from(value, sig):
    return sig * (1.0 + value * (1.0 - sig))


def matmul(left, right):
    return jnp.dot(left, right, preferred_element_type=F32)


def wait_for(ref, sem):
    pltpu.make_async_copy(ref, ref, sem).wait()


def send(src, dst, send_sem, recv_sem, **where):
    pltpu.make_async_remote_copy(
        src_ref=src,
        dst_ref=dst,
        send_sem=send_sem,
        recv_sem=recv_sem,
        device_id=where,
        device_id_type=MESH,
    ).start()


def kernel(
    nz, nx, ncol,
    count, features, upstream_hbm, tiles_hbm, rows_hbm, cols_hbm,
    w_one_hbm, b_one_hbm, w_two_hbm, b_two_hbm,
    hidden_out, grad_w_one, grad_b_one, grad_w_two, grad_b_two,
    tiles, dense, dense_t, gz_x, gx_x, gz_a, gx_a, agg_t, slope, hid, acc_one, acc_two,
    part_one, land_one, part_two, land_two, back,
    gone, piece_one, land_p1, z_p1, full_p1, piece_two, land_p2, z_p2, full_p2,
    bias_c, bias_x, bias_z, acc_w, acc_b, agg_h, agg_ht, grad_h, local_two,
    upstream, w_one, b_one, w_two, b_two, rows_of, cols_of, slots_vmem, slot_of,
    tile_sem, in_sem, ssem, recv_x, recv_a, recv_c, recv_back, recv_w,
):
    nrow = nz * nx
    slots = tiles.shape[0] - 1
    width = features.shape[1]
    hidden = w_one.shape[1]
    far_first = [nz // 2] + [d * g for d in range(nz // 2 - 1, 0, -1) for g in (1, -1)]
    row = lax.axis_index("row")
    col = lax.axis_index("col")
    mz = row // nx
    mx = lax.rem(row, nx)
    group = mx * ncol + col
    ngroup = nx * ncol
    cut = gz_x.shape[1]

    tile_copy = pltpu.make_async_copy(tiles_hbm.at[0, 0], tiles.at[pl.ds(0, slots)], tile_sem)
    own_copies = [
        pltpu.make_async_copy(src, dst, in_sem.at[k])
        for k, (src, dst) in enumerate((
            (rows_hbm.at[0], rows_of),
            (cols_hbm.at[0], cols_of),
            (features.at[pl.ds(0, cut)], gz_x.at[row]),
            (features.at[pl.ds(cut, 128 - cut)], gx_x.at[row]),
            (w_one_hbm, w_one),
            (b_one_hbm, b_one),
            (w_two_hbm, w_two),
            (b_two_hbm, b_two),
            (upstream_hbm, upstream),
        ))
    ]
    for copy in own_copies:
        copy.start()

    barrier = pltpu.get_barrier_semaphore()

    def member(d):
        to = lax.rem(group + d, ngroup)
        return to, {"row": mz * nx + to // ncol, "col": lax.rem(to, ncol)}

    @pl.loop(1, nz)
    def _(d):
        pl.semaphore_signal(
            barrier, inc=1, device_id={"row": lax.rem(mz + d, nz) * nx + mx}, device_id_type=MESH
        )

    @pl.loop(1, nrow)
    def _(d):
        pl.semaphore_signal(
            barrier, inc=1, device_id={"row": lax.rem(row + d, nrow)}, device_id_type=MESH
        )

    @pl.loop(1, ngroup)
    def _(d):
        pl.semaphore_signal(barrier, inc=1, device_id=member(d)[1], device_id_type=MESH)

    def peer_x(d):
        return lax.rem(mx + d, nx)

    def peer_z(d):
        return lax.rem(mz + d + nz, nz)

    def gather_row(by_z, by_x, own_z, own_x, rsem, ssem_, compute, placed, between):
        def push(buf, sems, first, number, z, x):
            part = buf.at[pl.ds(first, number)]
            send(part, part, ssem_, sems.at[first], row=z * nx + x)

        def push_own(buf, own, sems, z, x):
            send(own, buf.at[row], ssem_, sems.at[row], row=z * nx + x)

        def arrived(buf, sems, first, number):
            wait_for(buf.at[pl.ds(first, number)], sems.at[first])

        sems_z, sems_x = rsem.at[0], rsem.at[1]
        for d in range(1, nx):
            push_own(by_x, own_x, sems_x, mz, peer_x(d))
        for d in far_first[::-1]:
            push_own(by_z, own_z, sems_z, peer_z(d), mx)
        for d in range(1, nx):
            push_own(by_z, own_z, sems_z, mz, peer_x(d))
        placed()
        for d in range(1, nx):
            arrived(by_x, sems_x, mz * nx + peer_x(d), 1)
        for d in far_first[::-1]:
            push(by_x, sems_x, mz * nx, nx, peer_z(d), mx)

        def onward(d):
            at = peer_z(d) * nx + mx
            arrived(by_z, sems_z, at, 1)
            for e in range(1, nx):
                push(by_z, sems_z, at, 1, mz, peer_x(e))

        def use(d):
            zp = peer_z(d)

            @pl.loop(1, nx)
            def _(e):
                arrived(by_z, sems_z, zp * nx + peer_x(e), 1)

            compute(zp)

        near_first = far_first[::-1]
        early = len(near_first) // 2 + 1
        for d in near_first[:early]:
            onward(d)
        between()
        use(0)
        for d in near_first[early:]:
            onward(d)

        @pl.loop(1, nz)
        def _(q):
            d = ((q + 1) // 2) * (2 * lax.rem(q, 2) - 1)
            arrived(by_x, sems_x, peer_z(d) * nx, nx)
            use(d)

    def scatter_col(acc, part, land, rsem, ssem_):
        @pl.loop(1, ncol)
        def _(d):
            to = lax.rem(col + d, ncol)
            part[to] = acc[to].astype(BF)
            send(part.at[to], land.at[col], ssem_, rsem, col=to)

    def scattered_col(acc, land, rsem):
        wait_for(land.at[pl.ds(0, ncol - 1)], rsem)
        total = acc[col]
        for d in range(1, ncol):
            total = total + land[lax.rem(col + d, ncol)].astype(F32)
        return total.astype(BF)

    def own_placed():
        tile_copy.start()
        find_slots()
        own_copies[2].wait()
        own_copies[3].wait()

    def to_smem():
        return pltpu.make_async_copy(slots_vmem, slot_of, in_sem.at[0])

    def find_slots():
        own_copies[0].wait()
        own_copies[1].wait()
        places = ncol * nrow
        index = lax.broadcasted_iota(jnp.int32, (1, slots), 1)
        place = jnp.where(index < count[0, 0], rows_of[...] * nrow + cols_of[...], -1)
        column = jnp.broadcast_to(place, (8, slots)).T[:, :1]
        hit = column == lax.broadcasted_iota(jnp.int32, (slots, places), 1)
        entry = lax.broadcasted_iota(jnp.int32, (slots, places), 0) - slots
        found = jnp.sum(jnp.where(hit, entry, 0), axis=0, keepdims=True) + slots
        slots_vmem[...] = jnp.broadcast_to(found, slots_vmem.shape)
        to_smem().start()
        tiles[slots] = jnp.zeros(tiles.shape[1:], BF)
        acc_one[...] = jnp.zeros(acc_one.shape, F32)
        acc_two[...] = jnp.zeros(acc_two.shape, F32)

    def find_done():
        for copy in own_copies[4:]:
            copy.wait()
        to_smem().wait()
        tile_copy.wait()

    def build_dense(zp):
        for r in range(ncol):
            for x in range(nx):
                slot = jnp.clip(slot_of[0, r * nrow + zp * nx + x], 0, slots)
                dense[zp, pl.ds(r * 128, 128), pl.ds(x * 128, 128)] = tiles[slot]

    rows_step = min(1024, ncol * 128)

    def layer_one(zp):
        build_dense(zp)
        source = jnp.concatenate(
            [buf[zp * nx + x] for x in range(nx) for buf in (gz_x, gx_x)], axis=0
        )

        @pl.loop(0, ncol * 128 // rows_step)
        def _(m):
            at = pl.ds(pl.multiple_of(m * rows_step, rows_step), rows_step)
            more = matmul(dense[zp, at], source).reshape(rows_step // 128, 128, width)
            tiles_at = pl.ds(m * (rows_step // 128), rows_step // 128)
            acc_one[tiles_at] = acc_one[tiles_at] + more

    def layer_two(zp):
        for x in range(nx):
            source = jnp.concatenate([gz_a[zp * nx + x], gx_a[zp * nx + x]], axis=0)
            pre = matmul(source, w_one[...]) + b_one[...]
            sig = jax.nn.sigmoid(pre)
            at = pl.ds(x * 128, 128)
            slope[zp, at] = dsilu_from(pre, sig)
            hid[at] = (pre * sig).astype(BF)

        @pl.loop(0, ncol * 128 // rows_step)
        def _(m):
            at = pl.ds(pl.multiple_of(m * rows_step, rows_step), rows_step)
            more = matmul(dense[zp, at], hid[...]).reshape(rows_step // 128, 128, hidden)
            tiles_at = pl.ds(m * (rows_step // 128), rows_step // 128)
            acc_two[tiles_at] = acc_two[tiles_at] + more

    def set_own(by_z, by_x, value):
        by_z[row] = value[:cut]
        by_x[row] = value[cut:]

    pl.semaphore_wait(barrier, nz - 1 + ngroup - 1 + nrow - 1)

    gather_row(
        gz_x, gx_x, features.at[pl.ds(0, cut)], features.at[pl.ds(cut, 128 - cut)],
        recv_x, ssem.at[0], layer_one, own_placed, find_done,
    )


    scatter_col(acc_one, part_one, land_one, recv_c.at[0], ssem.at[1])

    @pl.loop(0, nz)
    def _(zp):
        for r in range(ncol):
            for x in range(nx):
                dense_t[zp, pl.ds(x * 128, 128), pl.ds(r * 128, 128)] = dense[
                    zp, pl.ds(r * 128, 128), pl.ds(x * 128, 128)
                ].T

    set_own(gz_a, gx_a, scattered_col(acc_one, land_one, recv_c.at[0]))

    gather_row(
        gz_a, gx_a, gz_a.at[row], gx_a.at[row], recv_a, ssem.at[2], layer_two,
        lambda: None, lambda: None,
    )


    my_y = col // 2
    core = lax.rem(col, 2)
    sibling = 1 - core
    twin = my_y * 2 + sibling
    ny = ncol // 2

    scatter_col(acc_two, part_two, land_two, recv_c.at[1], ssem.at[3])

    @pl.loop(0, nz)
    def _(zp):
        for x in range(nx):
            source = jnp.concatenate([gz_a[zp * nx + x], gx_a[zp * nx + x]], axis=0)
            agg_t[zp, :, pl.ds(x * 128, 128)] = source.T

    agg_h[...] = scattered_col(acc_two, land_two, recv_c.at[1])

    @pl.loop(0, 2)
    def _(m):
        at = pl.ds(pl.multiple_of(m * 64, 64), 64)
        pre = matmul(agg_h[at], w_two[...]) + b_two[...]
        sig = jax.nn.sigmoid(pre)
        hidden_out[at] = (pre * sig).astype(BF)
        grad = (upstream[at].astype(F32) * dsilu_from(pre, sig)).astype(BF)
        grad_h[at] = grad
        back[pl.ds(pl.multiple_of(col * 128 + m * 64, 64), 64)] = lax.dot_general(
            grad, w_two[...], (((1,), (1,)), ((), ())), preferred_element_type=F32
        ).astype(BF)

    def back_of(c):
        return back.at[pl.ds(pl.multiple_of(c * 128, 128), 128)]

    for d in range(1, ny):
        send(
            back_of(col), back_of(col), ssem.at[4], recv_back.at[col],
            col=2 * lax.rem(my_y + d, ny) + core,
        )
    send(back_of(col), back_of(col), ssem.at[4], recv_back.at[col], col=twin)

    for m in range(hidden // 128):
        agg_ht[m] = agg_h[:, m * 128 : m * 128 + 128].T

    @pl.loop(0, hidden // 128)
    def _(m):
        local_two[m] = matmul(agg_ht[m], grad_h[...])

    local_w_two = local_two[...].reshape(hidden, hidden)
    local_b_two = jnp.sum(grad_h[...].astype(F32), axis=0, keepdims=True)

    def tile_places(per):
        for t in range(ngroup * per // 8):
            r, c = t // (hidden // 128), t % (hidden // 128)
            yield t // (per // 8), pl.ds(t % (per // 8) * 8, 8), slice(r * 8, r * 8 + 8), slice(c * 128, c * 128 + 128)

    def split_pieces(piece, value):
        for n, at, r, c in tile_places(piece.shape[1]):
            piece[n, at] = value[r, c].astype(piece.dtype)

    def join_pieces(piece, out):
        for n, at, r, c in tile_places(piece.shape[1]):
            out[r, c] = piece[n, at]

    def spread_group(piece, land, send_sem, recv_sem):
        @pl.loop(1, ngroup)
        def _(d):
            to, where = member(d)
            send(piece.at[to], land.at[group], send_sem, recv_sem, **where)

        land[group] = piece[group]

    def gather_group(buf, send_sem, recv_sem):
        @pl.loop(1, ngroup)
        def _(d):
            send(buf.at[group], buf.at[group], send_sem, recv_sem, **member(d)[1])

    def share(buf, send_sem, recv_sem, me, where):
        @pl.loop(1, buf.shape[0])
        def _(d):
            send(
                buf.at[me], buf.at[me], send_sem, recv_sem,
                **where(lax.rem(me + d, buf.shape[0])),
            )

    def along_z(z):
        return {"row": z * nx + mx}

    def along_x(x):
        return {"row": mz * nx + x}

    def along_col(c):
        return {"col": c}

    def total(buf):
        value = buf[0].astype(F32)
        for k in range(1, buf.shape[0]):
            value = value + buf[k].astype(F32)
        return value

    def all_but_one(buf):
        return buf.at[pl.ds(0, buf.shape[0] - 1)]

    split_pieces(piece_two, local_w_two)
    for d in (1, 3, 2) if ny == 4 else range(1, ny):
        c = 2 * lax.rem(my_y + d, ny) + core
        wait_for(back_of(c), recv_back.at[c])
        send(back_of(c), back_of(c), ssem.at[14], recv_back.at[c], col=twin)
    spread_group(piece_two, land_p2, ssem.at[5], recv_w.at[0])
    for d in range(ny):
        c = 2 * lax.rem(my_y + d, ny) + sibling
        wait_for(back_of(c), recv_back.at[c])

    def backward(first, last):
        @pl.loop(first, last, step=2)
        def _(zp):
            for k in range(2):
                grad_one = (matmul(dense_t[zp + k], back[...]) * slope[zp + k]).astype(BF)
                gone[k] = grad_one
                acc_b[...] = acc_b[...] + jnp.sum(
                    grad_one.astype(F32).reshape(nx * 16, 8, hidden), axis=0
                )
            for k in range(2):
                acc_w[...] = acc_w[...] + matmul(agg_t[zp + k], gone[k])

    acc_w[...] = jnp.zeros(acc_w.shape, F32)
    acc_b[...] = jnp.zeros(acc_b.shape, F32)
    backward(0, nz // 2)
    wait_for(all_but_one(land_p2), recv_w.at[0])
    z_p2[mz] = total(land_p2)
    share(z_p2, ssem.at[6], recv_w.at[1], mz, along_z)
    backward(nz // 2, nz)

    split_pieces(piece_one, acc_w)
    spread_group(piece_one, land_p1, ssem.at[7], recv_w.at[2])
    local_b_one = jnp.sum(acc_b[...], axis=0, keepdims=True)
    for k, value in enumerate((local_b_one, local_b_two)):
        for c in range(hidden // 128):
            bias_z[mz, pl.ds(k * (hidden // 128) + c, 1)] = value[:, c * 128 : c * 128 + 128]
    share(bias_z, ssem.at[8], recv_w.at[3], mz, along_z)
    wait_for(all_but_one(z_p2), recv_w.at[1])
    full_p2[group] = total(z_p2)
    gather_group(full_p2, ssem.at[9], recv_w.at[4])

    wait_for(all_but_one(land_p1), recv_w.at[2])
    z_p1[mz] = total(land_p1)
    share(z_p1, ssem.at[10], recv_w.at[5], mz, along_z)
    wait_for(all_but_one(bias_z), recv_w.at[3])
    bias_x[mx] = total(bias_z)
    share(bias_x, ssem.at[11], recv_w.at[6], mx, along_x)

    wait_for(all_but_one(full_p2), recv_w.at[4])
    join_pieces(full_p2, grad_w_two)

    wait_for(all_but_one(z_p1), recv_w.at[5])
    full_p1[group] = total(z_p1)
    gather_group(full_p1, ssem.at[12], recv_w.at[7])
    wait_for(all_but_one(bias_x), recv_w.at[6])
    bias_c[col] = total(bias_x)
    share(bias_c, ssem.at[13], recv_w.at[8], col, along_col)

    wait_for(all_but_one(bias_c), recv_w.at[8])
    biases = total(bias_c)
    for k, out in enumerate((grad_b_one, grad_b_two)):
        for c in range(hidden // 128):
            at = k * (hidden // 128) + c
            out[:, pl.ds(c * 128, 128)] = biases[at : at + 1]
    wait_for(all_but_one(full_p1), recv_w.at[7])
    join_pieces(full_p1, grad_w_one)

    for k, buf in ((0, gz_x), (2, gz_a)):
        wait_for(buf.at[pl.ds(0, nrow - 1)], ssem.at[k])
    for k, buf in ((0, gx_x), (2, gx_a)):
        wait_for(buf.at[pl.ds(0, nrow - 1)], ssem.at[k])
    wait_for(all_but_one(part_one), ssem.at[1])
    wait_for(all_but_one(part_two), ssem.at[3])
    wait_for(back.at[pl.ds(0, ny * 128)], ssem.at[4])
    wait_for(back.at[pl.ds(0, (ny - 1) * 128)], ssem.at[14])
    for k, buf in enumerate(
        (piece_two, z_p2, piece_one, bias_z, full_p2, z_p1, bias_x, full_p1, bias_c)
    ):
        wait_for(all_but_one(buf), ssem.at[5 + k])


def hand_over(*refs):
    count = len(refs) // 2
    for src, dst in zip(refs[:count], refs[count:], strict=True):
        dst[...] = src[...]


def per_device(
    mesh_shape,
    features, upstream, tile_values, tile_rows, tile_cols, tile_count, w_one, b_one, w_two, b_two,
):
    nz, nx, ncol = mesh_shape
    nrow = nz * nx
    slots = tile_values.shape[2]
    width = features.shape[1]
    hidden = w_one.shape[1]
    ngroup = nx * ncol
    vmem = pl.BlockSpec(memory_space=pltpu.VMEM)
    anywhere = pl.BlockSpec(memory_space=pl.ANY)
    per_one = width * hidden // (8 * 128) // ngroup * 8
    per_two = hidden * hidden // (8 * 128) // ngroup * 8
    scratch = [
        pltpu.VMEM((slots + 1, 128, 128), BF),
        pltpu.VMEM((nz, ncol * 128, nx * 128), BF),
        pltpu.VMEM((nz, nx * 128, ncol * 128), BF),
        pltpu.VMEM((nrow, 96, width), BF),
        pltpu.VMEM((nrow, 32, width), BF),
        pltpu.VMEM((nrow, 96, width), BF),
        pltpu.VMEM((nrow, 32, width), BF),
        pltpu.VMEM((nz, width, nx * 128), BF),
        pltpu.VMEM((nz, nx * 128, hidden), F32),
        pltpu.VMEM((nx * 128, hidden), BF),
        pltpu.VMEM((ncol, 128, width), F32),
        pltpu.VMEM((ncol, 128, hidden), F32),
        pltpu.VMEM((ncol, 128, width), BF),
        pltpu.VMEM((ncol, 128, width), BF),
        pltpu.VMEM((ncol, 128, hidden), BF),
        pltpu.VMEM((ncol, 128, hidden), BF),
        pltpu.VMEM((ncol * 128, hidden), BF),
        pltpu.VMEM((2, nx * 128, hidden), BF),
        pltpu.VMEM((ngroup, per_one, 128), F32),
        pltpu.VMEM((ngroup, per_one, 128), F32),
        pltpu.VMEM((nz, per_one, 128), F32),
        pltpu.VMEM((ngroup, per_one, 128), F32),
        pltpu.VMEM((ngroup, per_two, 128), BF),
        pltpu.VMEM((ngroup, per_two, 128), BF),
        pltpu.VMEM((nz, per_two, 128), F32),
        pltpu.VMEM((ngroup, per_two, 128), F32),
        pltpu.VMEM((ncol, 8, 128), F32),
        pltpu.VMEM((nx, 8, 128), F32),
        pltpu.VMEM((nz, 8, 128), F32),
        pltpu.VMEM((width, hidden), F32),
        pltpu.VMEM((8, hidden), F32),
        pltpu.VMEM((128, hidden), BF),
        pltpu.VMEM((hidden // 128, 128, 128), BF),
        pltpu.VMEM((128, hidden), BF),
        pltpu.VMEM((hidden // 128, 128, hidden), F32),
        pltpu.VMEM((128, hidden), BF),
        pltpu.VMEM((width, hidden), BF),
        pltpu.VMEM((1, hidden), F32),
        pltpu.VMEM((hidden, hidden), BF),
        pltpu.VMEM((1, hidden), F32),
        pltpu.VMEM((1, slots), jnp.int32),
        pltpu.VMEM((1, slots), jnp.int32),
        pltpu.VMEM((8, ncol * nrow), jnp.int32),
        pltpu.SMEM((8, ncol * nrow), jnp.int32),
        pltpu.SemaphoreType.DMA,
        pltpu.SemaphoreType.DMA((9,)),
        pltpu.SemaphoreType.DMA((15,)),
        pltpu.SemaphoreType.DMA((2, nrow)),
        pltpu.SemaphoreType.DMA((2, nrow)),
        pltpu.SemaphoreType.DMA((2,)),
        pltpu.SemaphoreType.DMA((ncol,)),
        pltpu.SemaphoreType.DMA((9,)),
    ]
    out = pl.pallas_call(
        functools.partial(kernel, nz, nx, ncol),
        out_shape=(
            jax.ShapeDtypeStruct((128, hidden), BF),
            jax.ShapeDtypeStruct((width, hidden), F32),
            jax.ShapeDtypeStruct((1, hidden), F32),
            jax.ShapeDtypeStruct((hidden, hidden), F32),
            jax.ShapeDtypeStruct((1, hidden), F32),
        ),
        in_specs=[
            pl.BlockSpec(memory_space=pltpu.SMEM), *([anywhere] * 9),
        ],
        out_specs=(vmem,) * 5,
        scratch_shapes=scratch,
        compiler_params=pltpu.CompilerParams(
            collective_id=0, has_side_effects=True, vmem_limit_bytes=56 * 1024 * 1024
        ),
    )(
        tile_count, features, upstream, tile_values, tile_rows, tile_cols,
        w_one, b_one.reshape(1, hidden), w_two, b_two.reshape(1, hidden),
    )
    hidden_out, grad_w_one, grad_b_one, grad_w_two, grad_b_two = pl.pallas_call(
        hand_over,
        out_shape=tuple(jax.ShapeDtypeStruct(o.shape, o.dtype) for o in out),
        in_specs=[vmem] * 5,
        out_specs=(vmem,) * 5,
    )(*out)
    return (
        hidden_out, grad_w_one, grad_b_one.reshape(hidden), grad_w_two, grad_b_two.reshape(hidden)
    )


def solution(mesh, nx=4):
    nrow, ncol = mesh.shape["row"], mesh.shape["col"]
    in_specs = (
        P(("col", "row"), None),
        P(("col", "row"), None),
        P("row", "col", None, None, None),
        P("row", "col", None),
        P("row", "col", None),
        P("row", "col"),
        P(),
        P(),
        P(),
        P(),
    )
    out_specs = (P(("col", "row"), None), P(), P(), P(), P())
    return jax.shard_map(
        functools.partial(per_device, (nrow // nx, nx, ncol)),
        mesh=mesh, in_specs=in_specs, out_specs=out_specs, check_vma=False,
    )
```

```python
import functools

import jax
import jax.numpy as jnp
from jax import lax
from jax.experimental import pallas as pl
from jax.experimental.pallas import tpu as pltpu
from jax.sharding import PartitionSpec as P

MESH = pl.DeviceIdType.MESH
BF = jnp.bfloat16
F32 = jnp.float32


def dsilu_from(value, sig):
    return sig * (1.0 + value * (1.0 - sig))


def matmul(left, right):
    return jnp.dot(left, right, preferred_element_type=F32)


def wait_for(ref, sem):
    pltpu.make_async_copy(ref, ref, sem).wait()


def send(src, dst, send_sem, recv_sem, **where):
    pltpu.make_async_remote_copy(
        src_ref=src,
        dst_ref=dst,
        send_sem=send_sem,
        recv_sem=recv_sem,
        device_id=where,
        device_id_type=MESH,
    ).start()


def kernel(
    nz, nx, ncol,
    count, features, upstream_hbm, tiles_hbm, rows_hbm, cols_hbm,
    w_one_hbm, b_one_hbm, w_two_hbm, b_two_hbm,
    hidden_out, grad_w_one, grad_b_one, grad_w_two, grad_b_two,
    tiles, dense, dense_t, gz_x, gx_x, gz_a, gx_a, agg_t, slope, hid, acc_one, acc_two,
    part_one, land_one, part_two, land_two, back,
    gone, piece_one, land_p1, z_p1, full_p1, piece_two, land_p2, z_p2, full_p2,
    bias_c, bias_x, bias_z, acc_w, acc_b, agg_h, agg_ht, grad_h, local_two,
    upstream, w_one, b_one, w_two, b_two, rows_of, cols_of, slots_vmem, slot_of,
    tile_sem, in_sem, ssem, recv_x, recv_a, recv_c, recv_back, recv_w,
):
    nrow = nz * nx
    slots = tiles.shape[0] - 1
    width = features.shape[1]
    hidden = w_one.shape[1]
    far_first = [nz // 2] + [d * g for d in range(nz // 2 - 1, 0, -1) for g in (1, -1)]
    row = lax.axis_index("row")
    col = lax.axis_index("col")
    mz = row // nx
    mx = lax.rem(row, nx)
    group = mx * ncol + col
    ngroup = nx * ncol
    cut = gz_x.shape[1]

    tile_copy = pltpu.make_async_copy(tiles_hbm.at[0, 0], tiles.at[pl.ds(0, slots)], tile_sem)
    own_copies = [
        pltpu.make_async_copy(src, dst, in_sem.at[k])
        for k, (src, dst) in enumerate((
            (rows_hbm.at[0], rows_of),
            (cols_hbm.at[0], cols_of),
            (features.at[pl.ds(0, cut)], gz_x.at[row]),
            (features.at[pl.ds(cut, 128 - cut)], gx_x.at[row]),
            (w_one_hbm, w_one),
            (b_one_hbm, b_one),
            (w_two_hbm, w_two),
            (b_two_hbm, b_two),
            (upstream_hbm, upstream),
        ))
    ]
    for copy in own_copies:
        copy.start()

    barrier = pltpu.get_barrier_semaphore()

    def member(d):
        to = lax.rem(group + d, ngroup)
        return to, {"row": mz * nx + to // ncol, "col": lax.rem(to, ncol)}

    @pl.loop(1, nz)
    def _(d):
        pl.semaphore_signal(
            barrier, inc=1, device_id={"row": lax.rem(mz + d, nz) * nx + mx}, device_id_type=MESH
        )

    @pl.loop(1, nrow)
    def _(d):
        pl.semaphore_signal(
            barrier, inc=1, device_id={"row": lax.rem(row + d, nrow)}, device_id_type=MESH
        )

    @pl.loop(1, ngroup)
    def _(d):
        pl.semaphore_signal(barrier, inc=1, device_id=member(d)[1], device_id_type=MESH)

    def peer_x(d):
        return lax.rem(mx + d, nx)

    def peer_z(d):
        return lax.rem(mz + d + nz, nz)

    def gather_row(by_z, by_x, own_z, own_x, rsem, ssem_, compute, placed, between):
        def push(buf, sems, first, number, z, x):
            part = buf.at[pl.ds(first, number)]
            send(part, part, ssem_, sems.at[first], row=z * nx + x)

        def push_own(buf, own, sems, z, x):
            send(own, buf.at[row], ssem_, sems.at[row], row=z * nx + x)

        def arrived(buf, sems, first, number):
            wait_for(buf.at[pl.ds(first, number)], sems.at[first])

        sems_z, sems_x = rsem.at[0], rsem.at[1]
        for d in range(1, nx):
            push_own(by_x, own_x, sems_x, mz, peer_x(d))
        for d in far_first[::-1]:
            push_own(by_z, own_z, sems_z, peer_z(d), mx)
        for d in range(1, nx):
            push_own(by_z, own_z, sems_z, mz, peer_x(d))
        placed()
        for d in range(1, nx):
            arrived(by_x, sems_x, mz * nx + peer_x(d), 1)
        for d in far_first[::-1]:
            push(by_x, sems_x, mz * nx, nx, peer_z(d), mx)

        def onward(d):
            at = peer_z(d) * nx + mx
            arrived(by_z, sems_z, at, 1)
            for e in range(1, nx):
                push(by_z, sems_z, at, 1, mz, peer_x(e))

        def use(d):
            zp = peer_z(d)

            @pl.loop(1, nx)
            def _(e):
                arrived(by_z, sems_z, zp * nx + peer_x(e), 1)

            compute(zp)

        near_first = far_first[::-1]
        early = len(near_first) // 2 + 1
        for d in near_first[:early]:
            onward(d)
        between()
        use(0)
        for d in near_first[early:]:
            onward(d)

        @pl.loop(1, nz)
        def _(q):
            d = ((q + 1) // 2) * (2 * lax.rem(q, 2) - 1)
            arrived(by_x, sems_x, peer_z(d) * nx, nx)
            use(d)

    my_y = col // 2
    core = lax.rem(col, 2)
    ny = ncol // 2
    steps_y = sorted(range(1, ny), key=lambda d: -min(d, ny - d))
    col_order = [(d, c) for d in steps_y for c in (0, 1)] + [(0, 1)]

    def col_peer(d):
        other = core if d[1] == 0 else 1 - core
        return 2 * lax.rem(my_y + d[0], ny) + other

    def scatter_col(acc, part, land, rsem, ssem_):
        for d in col_order:
            to = col_peer(d)
            part[to] = acc[to].astype(BF)
            send(part.at[to], land.at[col], ssem_, rsem, col=to)

    def scattered_col(acc, land, rsem):
        wait_for(land.at[pl.ds(0, ncol - 1)], rsem)
        total = acc[col]
        for d in range(1, ncol):
            total = total + land[lax.rem(col + d, ncol)].astype(F32)
        return total.astype(BF)

    def own_placed():
        tile_copy.start()
        find_slots()
        own_copies[2].wait()
        own_copies[3].wait()

    def to_smem():
        return pltpu.make_async_copy(slots_vmem, slot_of, in_sem.at[0])

    def find_slots():
        own_copies[0].wait()
        own_copies[1].wait()
        places = ncol * nrow
        index = lax.broadcasted_iota(jnp.int32, (1, slots), 1)
        place = jnp.where(index < count[0, 0], rows_of[...] * nrow + cols_of[...], -1)
        column = jnp.broadcast_to(place, (8, slots)).T[:, :1]
        hit = column == lax.broadcasted_iota(jnp.int32, (slots, places), 1)
        entry = lax.broadcasted_iota(jnp.int32, (slots, places), 0) - slots
        found = jnp.sum(jnp.where(hit, entry, 0), axis=0, keepdims=True) + slots
        slots_vmem[...] = jnp.broadcast_to(found, slots_vmem.shape)
        to_smem().start()
        tiles[slots] = jnp.zeros(tiles.shape[1:], BF)
        acc_one[...] = jnp.zeros(acc_one.shape, F32)
        acc_two[...] = jnp.zeros(acc_two.shape, F32)

    def find_done():
        for copy in own_copies[4:]:
            copy.wait()
        to_smem().wait()
        tile_copy.wait()

    def build_dense(zp):
        for r in range(ncol):
            for x in range(nx):
                slot = jnp.clip(slot_of[0, r * nrow + zp * nx + x], 0, slots)
                dense[zp, pl.ds(r * 128, 128), pl.ds(x * 128, 128)] = tiles[slot]

    rows_step = min(1024, ncol * 128)

    def layer_one(zp):
        build_dense(zp)
        source = jnp.concatenate(
            [buf[zp * nx + x] for x in range(nx) for buf in (gz_x, gx_x)], axis=0
        )

        @pl.loop(0, ncol * 128 // rows_step)
        def _(m):
            at = pl.ds(pl.multiple_of(m * rows_step, rows_step), rows_step)
            more = matmul(dense[zp, at], source).reshape(rows_step // 128, 128, width)
            tiles_at = pl.ds(m * (rows_step // 128), rows_step // 128)
            acc_one[tiles_at] = acc_one[tiles_at] + more

    def layer_two(zp):
        for x in range(nx):
            source = jnp.concatenate([gz_a[zp * nx + x], gx_a[zp * nx + x]], axis=0)
            pre = matmul(source, w_one[...]) + b_one[...]
            sig = jax.nn.sigmoid(pre)
            at = pl.ds(x * 128, 128)
            slope[zp, at] = dsilu_from(pre, sig)
            hid[at] = (pre * sig).astype(BF)

        @pl.loop(0, ncol * 128 // rows_step)
        def _(m):
            at = pl.ds(pl.multiple_of(m * rows_step, rows_step), rows_step)
            more = matmul(dense[zp, at], hid[...]).reshape(rows_step // 128, 128, hidden)
            tiles_at = pl.ds(m * (rows_step // 128), rows_step // 128)
            acc_two[tiles_at] = acc_two[tiles_at] + more

    def set_own(by_z, by_x, value):
        by_z[row] = value[:cut]
        by_x[row] = value[cut:]

    pl.semaphore_wait(barrier, nz - 1 + ngroup - 1 + nrow - 1)

    gather_row(
        gz_x, gx_x, features.at[pl.ds(0, cut)], features.at[pl.ds(cut, 128 - cut)],
        recv_x, ssem.at[0], layer_one, own_placed, find_done,
    )


    scatter_col(acc_one, part_one, land_one, recv_c.at[0], ssem.at[1])

    @pl.loop(0, nz)
    def _(zp):
        for r in range(ncol):
            for x in range(nx):
                dense_t[zp, pl.ds(x * 128, 128), pl.ds(r * 128, 128)] = dense[
                    zp, pl.ds(r * 128, 128), pl.ds(x * 128, 128)
                ].T

    set_own(gz_a, gx_a, scattered_col(acc_one, land_one, recv_c.at[0]))

    gather_row(
        gz_a, gx_a, gz_a.at[row], gx_a.at[row], recv_a, ssem.at[2], layer_two,
        lambda: None, lambda: None,
    )


    scatter_col(acc_two, part_two, land_two, recv_c.at[1], ssem.at[3])

    @pl.loop(0, nz)
    def _(zp):
        for x in range(nx):
            source = jnp.concatenate([gz_a[zp * nx + x], gx_a[zp * nx + x]], axis=0)
            agg_t[zp, :, pl.ds(x * 128, 128)] = source.T

    agg_h[...] = scattered_col(acc_two, land_two, recv_c.at[1])

    @pl.loop(0, 1)
    def _(m):
        at = pl.ds(pl.multiple_of(m * 128, 128), 128)
        pre = matmul(agg_h[at], w_two[...]) + b_two[...]
        sig = jax.nn.sigmoid(pre)
        hidden_out[at] = (pre * sig).astype(BF)
        grad = (upstream[at].astype(F32) * dsilu_from(pre, sig)).astype(BF)
        grad_h[at] = grad
        back[pl.ds(pl.multiple_of((col + m) * 128, 128), 128)] = lax.dot_general(
            grad, w_two[...], (((1,), (1,)), ((), ())), preferred_element_type=F32
        ).astype(BF)

    def back_of(c):
        return back.at[pl.ds(pl.multiple_of(c * 128, 128), 128)]

    for d in col_order:
        send(back_of(col), back_of(col), ssem.at[4], recv_back.at[0], col=col_peer(d))

    for m in range(hidden // 128):
        agg_ht[m] = agg_h[:, m * 128 : m * 128 + 128].T

    @pl.loop(0, hidden // 128)
    def _(m):
        local_two[m] = matmul(agg_ht[m], grad_h[...])

    local_w_two = local_two[...].reshape(hidden, hidden)
    local_b_two = jnp.sum(grad_h[...].astype(F32), axis=0, keepdims=True)

    def tile_places(per):
        for t in range(ngroup * per // 8):
            r, c = t // (hidden // 128), t % (hidden // 128)
            yield t // (per // 8), pl.ds(t % (per // 8) * 8, 8), slice(r * 8, r * 8 + 8), slice(c * 128, c * 128 + 128)

    def split_pieces(piece, value):
        for n, at, r, c in tile_places(piece.shape[1]):
            piece[n, at] = value[r, c].astype(piece.dtype)

    def join_pieces(piece, out):
        for n, at, r, c in tile_places(piece.shape[1]):
            out[r, c] = piece[n, at]

    def spread_group(piece, land, send_sem, recv_sem):
        @pl.loop(1, ngroup)
        def _(d):
            to, where = member(d)
            send(piece.at[to], land.at[group], send_sem, recv_sem, **where)

        land[group] = piece[group]

    def gather_group(buf, send_sem, recv_sem):
        @pl.loop(1, ngroup)
        def _(d):
            send(buf.at[group], buf.at[group], send_sem, recv_sem, **member(d)[1])

    def share(buf, send_sem, recv_sem, me, where):
        @pl.loop(1, buf.shape[0])
        def _(d):
            send(
                buf.at[me], buf.at[me], send_sem, recv_sem,
                **where(lax.rem(me + d, buf.shape[0])),
            )

    def along_z(z):
        return {"row": z * nx + mx}

    def along_x(x):
        return {"row": mz * nx + x}

    def along_col(c):
        return {"col": c}

    def total(buf):
        value = buf[0].astype(F32)
        for k in range(1, buf.shape[0]):
            value = value + buf[k].astype(F32)
        return value

    def all_but_one(buf):
        return buf.at[pl.ds(0, buf.shape[0] - 1)]

    split_pieces(piece_two, local_w_two)
    spread_group(piece_two, land_p2, ssem.at[5], recv_w.at[0])
    wait_for(back.at[pl.ds(0, (ncol - 1) * 128)], recv_back.at[0])

    per_step = gone.shape[0]

    def backward(first, last):
        @pl.loop(first, last, step=per_step)
        def _(zp):
            for k in range(per_step):
                grad_one = (matmul(dense_t[zp + k], back[...]) * slope[zp + k]).astype(BF)
                gone[k] = grad_one
                acc_b[...] = acc_b[...] + jnp.sum(
                    grad_one.astype(F32).reshape(nx * 16, 8, hidden), axis=0
                )
            for k in range(per_step):
                acc_w[...] = acc_w[...] + matmul(agg_t[zp + k], gone[k])

    acc_w[...] = jnp.zeros(acc_w.shape, F32)
    acc_b[...] = jnp.zeros(acc_b.shape, F32)
    backward(0, nz // 2)
    wait_for(all_but_one(land_p2), recv_w.at[0])
    z_p2[mz] = total(land_p2)
    share(z_p2, ssem.at[6], recv_w.at[1], mz, along_z)
    backward(nz // 2, nz)

    split_pieces(piece_one, acc_w)
    spread_group(piece_one, land_p1, ssem.at[7], recv_w.at[2])
    local_b_one = jnp.sum(acc_b[...], axis=0, keepdims=True)
    for k, value in enumerate((local_b_one, local_b_two)):
        for c in range(hidden // 128):
            bias_z[mz, pl.ds(k * (hidden // 128) + c, 1)] = value[:, c * 128 : c * 128 + 128]
    share(bias_z, ssem.at[8], recv_w.at[3], mz, along_z)
    wait_for(all_but_one(z_p2), recv_w.at[1])
    full_p2[group] = total(z_p2)
    gather_group(full_p2, ssem.at[9], recv_w.at[4])

    wait_for(all_but_one(land_p1), recv_w.at[2])
    z_p1[mz] = total(land_p1)
    share(z_p1, ssem.at[10], recv_w.at[5], mz, along_z)
    wait_for(all_but_one(bias_z), recv_w.at[3])
    bias_x[mx] = total(bias_z)
    share(bias_x, ssem.at[11], recv_w.at[6], mx, along_x)

    wait_for(all_but_one(full_p2), recv_w.at[4])
    join_pieces(full_p2, grad_w_two)

    wait_for(all_but_one(z_p1), recv_w.at[5])
    full_p1[group] = total(z_p1)
    gather_group(full_p1, ssem.at[12], recv_w.at[7])
    wait_for(all_but_one(bias_x), recv_w.at[6])
    bias_c[col] = total(bias_x)
    share(bias_c, ssem.at[13], recv_w.at[8], col, along_col)

    wait_for(all_but_one(bias_c), recv_w.at[8])
    biases = total(bias_c)
    for k, out in enumerate((grad_b_one, grad_b_two)):
        for c in range(hidden // 128):
            at = k * (hidden // 128) + c
            out[:, pl.ds(c * 128, 128)] = biases[at : at + 1]
    wait_for(all_but_one(full_p1), recv_w.at[7])
    join_pieces(full_p1, grad_w_one)

    for k, buf in ((0, gz_x), (2, gz_a)):
        wait_for(buf.at[pl.ds(0, nrow - 1)], ssem.at[k])
    for k, buf in ((0, gx_x), (2, gx_a)):
        wait_for(buf.at[pl.ds(0, nrow - 1)], ssem.at[k])
    wait_for(all_but_one(part_one), ssem.at[1])
    wait_for(all_but_one(part_two), ssem.at[3])
    wait_for(back.at[pl.ds(0, (ncol - 1) * 128)], ssem.at[4])
    for k, buf in enumerate(
        (piece_two, z_p2, piece_one, bias_z, full_p2, z_p1, bias_x, full_p1, bias_c)
    ):
        wait_for(all_but_one(buf), ssem.at[5 + k])


def hand_over(*refs):
    count = len(refs) // 2
    for src, dst in zip(refs[:count], refs[count:], strict=True):
        dst[...] = src[...]


def per_device(
    mesh_shape,
    features, upstream, tile_values, tile_rows, tile_cols, tile_count, w_one, b_one, w_two, b_two,
):
    nz, nx, ncol = mesh_shape
    nrow = nz * nx
    slots = tile_values.shape[2]
    width = features.shape[1]
    hidden = w_one.shape[1]
    ngroup = nx * ncol
    vmem = pl.BlockSpec(memory_space=pltpu.VMEM)
    anywhere = pl.BlockSpec(memory_space=pl.ANY)
    per_one = width * hidden // (8 * 128) // ngroup * 8
    per_two = hidden * hidden // (8 * 128) // ngroup * 8
    scratch = [
        pltpu.VMEM((slots + 1, 128, 128), BF),
        pltpu.VMEM((nz, ncol * 128, nx * 128), BF),
        pltpu.VMEM((nz, nx * 128, ncol * 128), BF),
        pltpu.VMEM((nrow, 96, width), BF),
        pltpu.VMEM((nrow, 32, width), BF),
        pltpu.VMEM((nrow, 96, width), BF),
        pltpu.VMEM((nrow, 32, width), BF),
        pltpu.VMEM((nz, width, nx * 128), BF),
        pltpu.VMEM((nz, nx * 128, hidden), F32),
        pltpu.VMEM((nx * 128, hidden), BF),
        pltpu.VMEM((ncol, 128, width), F32),
        pltpu.VMEM((ncol, 128, hidden), F32),
        pltpu.VMEM((ncol, 128, width), BF),
        pltpu.VMEM((ncol, 128, width), BF),
        pltpu.VMEM((ncol, 128, hidden), BF),
        pltpu.VMEM((ncol, 128, hidden), BF),
        pltpu.VMEM((ncol * 128, hidden), BF),
        pltpu.VMEM((nz // 2, nx * 128, hidden), BF),
        pltpu.VMEM((ngroup, per_one, 128), F32),
        pltpu.VMEM((ngroup, per_one, 128), F32),
        pltpu.VMEM((nz, per_one, 128), F32),
        pltpu.VMEM((ngroup, per_one, 128), F32),
        pltpu.VMEM((ngroup, per_two, 128), BF),
        pltpu.VMEM((ngroup, per_two, 128), BF),
        pltpu.VMEM((nz, per_two, 128), F32),
        pltpu.VMEM((ngroup, per_two, 128), F32),
        pltpu.VMEM((ncol, 8, 128), F32),
        pltpu.VMEM((nx, 8, 128), F32),
        pltpu.VMEM((nz, 8, 128), F32),
        pltpu.VMEM((width, hidden), F32),
        pltpu.VMEM((8, hidden), F32),
        pltpu.VMEM((128, hidden), BF),
        pltpu.VMEM((hidden // 128, 128, 128), BF),
        pltpu.VMEM((128, hidden), BF),
        pltpu.VMEM((hidden // 128, 128, hidden), F32),
        pltpu.VMEM((128, hidden), BF),
        pltpu.VMEM((width, hidden), BF),
        pltpu.VMEM((1, hidden), F32),
        pltpu.VMEM((hidden, hidden), BF),
        pltpu.VMEM((1, hidden), F32),
        pltpu.VMEM((1, slots), jnp.int32),
        pltpu.VMEM((1, slots), jnp.int32),
        pltpu.VMEM((8, ncol * nrow), jnp.int32),
        pltpu.SMEM((8, ncol * nrow), jnp.int32),
        pltpu.SemaphoreType.DMA,
        pltpu.SemaphoreType.DMA((9,)),
        pltpu.SemaphoreType.DMA((15,)),
        pltpu.SemaphoreType.DMA((2, nrow)),
        pltpu.SemaphoreType.DMA((2, nrow)),
        pltpu.SemaphoreType.DMA((2,)),
        pltpu.SemaphoreType.DMA((ncol,)),
        pltpu.SemaphoreType.DMA((9,)),
    ]
    out = pl.pallas_call(
        functools.partial(kernel, nz, nx, ncol),
        out_shape=(
            jax.ShapeDtypeStruct((128, hidden), BF),
            jax.ShapeDtypeStruct((width, hidden), F32),
            jax.ShapeDtypeStruct((1, hidden), F32),
            jax.ShapeDtypeStruct((hidden, hidden), F32),
            jax.ShapeDtypeStruct((1, hidden), F32),
        ),
        in_specs=[
            pl.BlockSpec(memory_space=pltpu.SMEM), *([anywhere] * 9),
        ],
        out_specs=(vmem,) * 5,
        scratch_shapes=scratch,
        compiler_params=pltpu.CompilerParams(
            collective_id=0, has_side_effects=True, vmem_limit_bytes=56 * 1024 * 1024
        ),
    )(
        tile_count, features, upstream, tile_values, tile_rows, tile_cols,
        w_one, b_one.reshape(1, hidden), w_two, b_two.reshape(1, hidden),
    )
    hidden_out, grad_w_one, grad_b_one, grad_w_two, grad_b_two = pl.pallas_call(
        hand_over,
        out_shape=tuple(jax.ShapeDtypeStruct(o.shape, o.dtype) for o in out),
        in_specs=[vmem] * 5,
        out_specs=(vmem,) * 5,
    )(*out)
    return (
        hidden_out, grad_w_one, grad_b_one.reshape(hidden), grad_w_two, grad_b_two.reshape(hidden)
    )


def solution(mesh, nx=4):
    nrow, ncol = mesh.shape["row"], mesh.shape["col"]
    in_specs = (
        P(("col", "row"), None),
        P(("col", "row"), None),
        P("row", "col", None, None, None),
        P("row", "col", None),
        P("row", "col", None),
        P("row", "col"),
        P(),
        P(),
        P(),
        P(),
    )
    out_specs = (P(("col", "row"), None), P(), P(), P(), P())
    return jax.shard_map(
        functools.partial(per_device, (nrow // nx, nx, ncol)),
        mesh=mesh, in_specs=in_specs, out_specs=out_specs, check_vma=False,
    )
```

```python
import functools

import jax
import jax.numpy as jnp
from jax import lax
from jax.experimental import pallas as pl
from jax.experimental.pallas import tpu as pltpu
from jax.sharding import PartitionSpec as P

MESH = pl.DeviceIdType.MESH
BF = jnp.bfloat16
F32 = jnp.float32


def dsilu_from(value, sig):
    return sig * (1.0 + value * (1.0 - sig))


def matmul(left, right):
    return jnp.dot(left, right, preferred_element_type=F32)


def wait_for(ref, sem):
    pltpu.make_async_copy(ref, ref, sem).wait()


def send(src, dst, send_sem, recv_sem, **where):
    pltpu.make_async_remote_copy(
        src_ref=src,
        dst_ref=dst,
        send_sem=send_sem,
        recv_sem=recv_sem,
        device_id=where,
        device_id_type=MESH,
    ).start()


def kernel(
    nz, nx, ncol,
    count, features, upstream_hbm, tiles_hbm, rows_hbm, cols_hbm,
    w_one_hbm, b_one_hbm, w_two_hbm, b_two_hbm,
    hidden_out, grad_w_one, grad_b_one, grad_w_two, grad_b_two,
    tiles, dense, dense_t, gz_x, gx_x, gz_a, gx_a, agg_t, slope, hid, acc_one, acc_two,
    part_one, land_one, part_two, land_two, back,
    gone, piece_one, land_p1, z_p1, full_p1, piece_two, land_p2, z_p2, full_p2,
    bias_c, bias_x, bias_z, acc_w, acc_b, agg_h, agg_ht, grad_h, local_two,
    upstream, w_one, b_one, w_two, b_two, rows_of, cols_of, slots_vmem, slot_of,
    tile_sem, in_sem, ssem, recv_x, recv_a, recv_c, recv_back, recv_w,
):
    nrow = nz * nx
    slots = tiles.shape[0] - 1
    width = features.shape[1]
    hidden = w_one.shape[1]
    far_first = [nz // 2] + [d * g for d in range(nz // 2 - 1, 0, -1) for g in (1, -1)]
    row = lax.axis_index("row")
    col = lax.axis_index("col")
    mz = row // nx
    mx = lax.rem(row, nx)
    group = mx * ncol + col
    ngroup = nx * ncol
    cut = gz_x.shape[1]

    tile_copy = pltpu.make_async_copy(tiles_hbm.at[0, 0], tiles.at[pl.ds(0, slots)], tile_sem)
    own_copies = [
        pltpu.make_async_copy(src, dst, in_sem.at[k])
        for k, (src, dst) in enumerate((
            (rows_hbm.at[0], rows_of),
            (cols_hbm.at[0], cols_of),
            (features.at[pl.ds(0, cut)], gz_x.at[row]),
            (features.at[pl.ds(cut, 128 - cut)], gx_x.at[row]),
            (w_one_hbm, w_one),
            (b_one_hbm, b_one),
            (w_two_hbm, w_two),
            (b_two_hbm, b_two),
            (upstream_hbm, upstream),
        ))
    ]
    for copy in own_copies:
        copy.start()

    barrier = pltpu.get_barrier_semaphore()

    def member(d):
        to = lax.rem(group + d, ngroup)
        return to, {"row": mz * nx + to // ncol, "col": lax.rem(to, ncol)}

    @pl.loop(1, nz)
    def _(d):
        pl.semaphore_signal(
            barrier, inc=1, device_id={"row": lax.rem(mz + d, nz) * nx + mx}, device_id_type=MESH
        )

    @pl.loop(1, nrow)
    def _(d):
        pl.semaphore_signal(
            barrier, inc=1, device_id={"row": lax.rem(row + d, nrow)}, device_id_type=MESH
        )

    @pl.loop(1, ngroup)
    def _(d):
        pl.semaphore_signal(barrier, inc=1, device_id=member(d)[1], device_id_type=MESH)

    def peer_x(d):
        return lax.rem(mx + d, nx)

    def peer_z(d):
        return lax.rem(mz + d + nz, nz)

    def gather_row(by_z, by_x, own_z, own_x, rsem, ssem_, compute, placed, between):
        def push(buf, sems, first, number, z, x):
            part = buf.at[pl.ds(first, number)]
            send(part, part, ssem_, sems.at[first], row=z * nx + x)

        def push_own(buf, own, sems, z, x):
            send(own, buf.at[row], ssem_, sems.at[row], row=z * nx + x)

        def arrived(buf, sems, first, number):
            wait_for(buf.at[pl.ds(first, number)], sems.at[first])

        sems_z, sems_x = rsem.at[0], rsem.at[1]
        for d in range(1, nx):
            push_own(by_x, own_x, sems_x, mz, peer_x(d))
        for d in far_first[::-1]:
            push_own(by_z, own_z, sems_z, peer_z(d), mx)
        for d in range(1, nx):
            push_own(by_z, own_z, sems_z, mz, peer_x(d))
        placed()
        for d in range(1, nx):
            arrived(by_x, sems_x, mz * nx + peer_x(d), 1)
        for d in far_first[::-1]:
            push(by_x, sems_x, mz * nx, nx, peer_z(d), mx)

        def onward(d):
            at = peer_z(d) * nx + mx
            arrived(by_z, sems_z, at, 1)
            for e in range(1, nx):
                push(by_z, sems_z, at, 1, mz, peer_x(e))

        def use(d):
            zp = peer_z(d)

            @pl.loop(1, nx)
            def _(e):
                arrived(by_z, sems_z, zp * nx + peer_x(e), 1)

            compute(zp)

        near_first = far_first[::-1]
        for d in near_first:
            onward(d)
        between()
        use(0)

        @pl.loop(1, nz)
        def _(q):
            d = ((q + 1) // 2) * (2 * lax.rem(q, 2) - 1)
            arrived(by_x, sems_x, peer_z(d) * nx, nx)
            use(d)

    my_y = col // 2
    core = lax.rem(col, 2)
    ny = ncol // 2
    steps_y = sorted(range(1, ny), key=lambda d: -min(d, ny - d))
    col_order = [(d, c) for d in steps_y for c in (0, 1)] + [(0, 1)]

    def col_peer(d):
        other = core if d[1] == 0 else 1 - core
        return 2 * lax.rem(my_y + d[0], ny) + other

    def scatter_col(acc, part, land, rsem, ssem_):
        for d in col_order:
            to = col_peer(d)
            part[to] = acc[to].astype(BF)
            send(part.at[to], land.at[col], ssem_, rsem, col=to)

    def scattered_col(acc, land, rsem):
        wait_for(land.at[pl.ds(0, ncol - 1)], rsem)
        total = acc[col]
        for d in range(1, ncol):
            total = total + land[lax.rem(col + d, ncol)].astype(F32)
        return total.astype(BF)

    def own_placed():
        tile_copy.start()
        find_slots()
        own_copies[2].wait()
        own_copies[3].wait()

    def to_smem():
        return pltpu.make_async_copy(slots_vmem, slot_of, in_sem.at[0])

    def find_slots():
        own_copies[0].wait()
        own_copies[1].wait()
        places = ncol * nrow
        index = lax.broadcasted_iota(jnp.int32, (1, slots), 1)
        place = jnp.where(index < count[0, 0], rows_of[...] * nrow + cols_of[...], -1)
        column = jnp.broadcast_to(place, (8, slots)).T[:, :1]
        hit = column == lax.broadcasted_iota(jnp.int32, (slots, places), 1)
        entry = lax.broadcasted_iota(jnp.int32, (slots, places), 0) - slots
        found = jnp.sum(jnp.where(hit, entry, 0), axis=0, keepdims=True) + slots
        slots_vmem[...] = jnp.broadcast_to(found, slots_vmem.shape)
        to_smem().start()
        tiles[slots] = jnp.zeros(tiles.shape[1:], BF)
        acc_one[...] = jnp.zeros(acc_one.shape, F32)
        acc_two[...] = jnp.zeros(acc_two.shape, F32)

    def find_done():
        for copy in own_copies[4:]:
            copy.wait()
        to_smem().wait()
        tile_copy.wait()

    def build_dense(zp):
        for r in range(ncol):
            for x in range(nx):
                slot = jnp.clip(slot_of[0, r * nrow + zp * nx + x], 0, slots)
                dense[zp, pl.ds(r * 128, 128), pl.ds(x * 128, 128)] = tiles[slot]

    rows_step = min(1024, ncol * 128)

    def layer_one(zp):
        build_dense(zp)
        source = jnp.concatenate(
            [buf[zp * nx + x] for x in range(nx) for buf in (gz_x, gx_x)], axis=0
        )

        @pl.loop(0, ncol * 128 // rows_step)
        def _(m):
            at = pl.ds(pl.multiple_of(m * rows_step, rows_step), rows_step)
            more = matmul(dense[zp, at], source).reshape(rows_step // 128, 128, width)
            tiles_at = pl.ds(m * (rows_step // 128), rows_step // 128)
            acc_one[tiles_at] = acc_one[tiles_at] + more

    def layer_two(zp):
        for x in range(nx):
            source = jnp.concatenate([gz_a[zp * nx + x], gx_a[zp * nx + x]], axis=0)
            pre = matmul(source, w_one[...]) + b_one[...]
            sig = jax.nn.sigmoid(pre)
            at = pl.ds(x * 128, 128)
            slope[zp, at] = dsilu_from(pre, sig)
            hid[at] = (pre * sig).astype(BF)

        @pl.loop(0, ncol * 128 // rows_step)
        def _(m):
            at = pl.ds(pl.multiple_of(m * rows_step, rows_step), rows_step)
            more = matmul(dense[zp, at], hid[...]).reshape(rows_step // 128, 128, hidden)
            tiles_at = pl.ds(m * (rows_step // 128), rows_step // 128)
            acc_two[tiles_at] = acc_two[tiles_at] + more

    def set_own(by_z, by_x, value):
        by_z[row] = value[:cut]
        by_x[row] = value[cut:]

    pl.semaphore_wait(barrier, nz - 1 + ngroup - 1 + nrow - 1)

    gather_row(
        gz_x, gx_x, features.at[pl.ds(0, cut)], features.at[pl.ds(cut, 128 - cut)],
        recv_x, ssem.at[0], layer_one, own_placed, find_done,
    )


    scatter_col(acc_one, part_one, land_one, recv_c.at[0], ssem.at[1])

    @pl.loop(0, nz)
    def _(zp):
        for r in range(ncol):
            for x in range(nx):
                dense_t[zp, pl.ds(x * 128, 128), pl.ds(r * 128, 128)] = dense[
                    zp, pl.ds(r * 128, 128), pl.ds(x * 128, 128)
                ].T

    set_own(gz_a, gx_a, scattered_col(acc_one, land_one, recv_c.at[0]))

    gather_row(
        gz_a, gx_a, gz_a.at[row], gx_a.at[row], recv_a, ssem.at[2], layer_two,
        lambda: None, lambda: None,
    )


    scatter_col(acc_two, part_two, land_two, recv_c.at[1], ssem.at[3])

    @pl.loop(0, nz)
    def _(zp):
        for x in range(nx):
            source = jnp.concatenate([gz_a[zp * nx + x], gx_a[zp * nx + x]], axis=0)
            agg_t[zp, :, pl.ds(x * 128, 128)] = source.T

    agg_h[...] = scattered_col(acc_two, land_two, recv_c.at[1])

    @pl.loop(0, 1)
    def _(m):
        at = pl.ds(pl.multiple_of(m * 128, 128), 128)
        pre = matmul(agg_h[at], w_two[...]) + b_two[...]
        sig = jax.nn.sigmoid(pre)
        hidden_out[at] = (pre * sig).astype(BF)
        grad = (upstream[at].astype(F32) * dsilu_from(pre, sig)).astype(BF)
        grad_h[at] = grad
        back[pl.ds(pl.multiple_of((col + m) * 128, 128), 128)] = lax.dot_general(
            grad, w_two[...], (((1,), (1,)), ((), ())), preferred_element_type=F32
        ).astype(BF)

    def back_of(c):
        return back.at[pl.ds(pl.multiple_of(c * 128, 128), 128)]

    for d in col_order:
        send(back_of(col), back_of(col), ssem.at[4], recv_back.at[0], col=col_peer(d))

    for m in range(hidden // 128):
        agg_ht[m] = agg_h[:, m * 128 : m * 128 + 128].T

    @pl.loop(0, hidden // 128)
    def _(m):
        local_two[m] = matmul(agg_ht[m], grad_h[...])

    local_w_two = local_two[...].reshape(hidden, hidden)
    local_b_two = jnp.sum(grad_h[...].astype(F32), axis=0, keepdims=True)

    def tile_places(per):
        for t in range(ngroup * per // 8):
            r, c = t // (hidden // 128), t % (hidden // 128)
            yield t // (per // 8), pl.ds(t % (per // 8) * 8, 8), slice(r * 8, r * 8 + 8), slice(c * 128, c * 128 + 128)

    def split_pieces(piece, value):
        for n, at, r, c in tile_places(piece.shape[1]):
            piece[n, at] = value[r, c].astype(piece.dtype)

    def join_pieces(piece, out):
        for n, at, r, c in tile_places(piece.shape[1]):
            out[r, c] = piece[n, at]

    def spread_group(piece, land, send_sem, recv_sem):
        @pl.loop(1, ngroup)
        def _(d):
            to, where = member(d)
            send(piece.at[to], land.at[group], send_sem, recv_sem, **where)

        land[group] = piece[group]

    def gather_group(buf, send_sem, recv_sem):
        @pl.loop(1, ngroup)
        def _(d):
            send(buf.at[group], buf.at[group], send_sem, recv_sem, **member(d)[1])

    def share(buf, send_sem, recv_sem, me, where):
        @pl.loop(1, buf.shape[0])
        def _(d):
            send(
                buf.at[me], buf.at[me], send_sem, recv_sem,
                **where(lax.rem(me + d, buf.shape[0])),
            )

    def along_z(z):
        return {"row": z * nx + mx}

    def along_x(x):
        return {"row": mz * nx + x}

    def along_col(c):
        return {"col": c}

    def total(buf):
        value = buf[0].astype(F32)
        for k in range(1, buf.shape[0]):
            value = value + buf[k].astype(F32)
        return value

    def all_but_one(buf):
        return buf.at[pl.ds(0, buf.shape[0] - 1)]

    split_pieces(piece_two, local_w_two)
    spread_group(piece_two, land_p2, ssem.at[5], recv_w.at[0])
    wait_for(back.at[pl.ds(0, (ncol - 1) * 128)], recv_back.at[0])

    per_step = gone.shape[0]

    def backward(first, last):
        @pl.loop(first, last, step=per_step)
        def _(zp):
            for k in range(per_step):
                grad_one = (matmul(dense_t[zp + k], back[...]) * slope[zp + k]).astype(BF)
                gone[k] = grad_one
                acc_b[...] = acc_b[...] + jnp.sum(
                    grad_one.astype(F32).reshape(nx * 16, 8, hidden), axis=0
                )
            for k in range(per_step):
                acc_w[...] = acc_w[...] + matmul(agg_t[zp + k], gone[k])

    acc_w[...] = jnp.zeros(acc_w.shape, F32)
    acc_b[...] = jnp.zeros(acc_b.shape, F32)
    backward(0, nz // 2)
    wait_for(all_but_one(land_p2), recv_w.at[0])
    z_p2[mz] = total(land_p2)
    share(z_p2, ssem.at[6], recv_w.at[1], mz, along_z)
    backward(nz // 2, nz)

    split_pieces(piece_one, acc_w)
    spread_group(piece_one, land_p1, ssem.at[7], recv_w.at[2])
    local_b_one = jnp.sum(acc_b[...], axis=0, keepdims=True)
    for k, value in enumerate((local_b_one, local_b_two)):
        for c in range(hidden // 128):
            bias_z[mz, pl.ds(k * (hidden // 128) + c, 1)] = value[:, c * 128 : c * 128 + 128]
    share(bias_z, ssem.at[8], recv_w.at[3], mz, along_z)
    wait_for(all_but_one(z_p2), recv_w.at[1])
    full_p2[group] = total(z_p2)
    gather_group(full_p2, ssem.at[9], recv_w.at[4])

    wait_for(all_but_one(land_p1), recv_w.at[2])
    z_p1[mz] = total(land_p1)
    share(z_p1, ssem.at[10], recv_w.at[5], mz, along_z)
    wait_for(all_but_one(bias_z), recv_w.at[3])
    bias_x[mx] = total(bias_z)
    share(bias_x, ssem.at[11], recv_w.at[6], mx, along_x)

    wait_for(all_but_one(full_p2), recv_w.at[4])
    join_pieces(full_p2, grad_w_two)

    wait_for(all_but_one(z_p1), recv_w.at[5])
    full_p1[group] = total(z_p1)
    gather_group(full_p1, ssem.at[12], recv_w.at[7])
    wait_for(all_but_one(bias_x), recv_w.at[6])
    bias_c[col] = total(bias_x)
    share(bias_c, ssem.at[13], recv_w.at[8], col, along_col)

    wait_for(all_but_one(bias_c), recv_w.at[8])
    biases = total(bias_c)
    for k, out in enumerate((grad_b_one, grad_b_two)):
        for c in range(hidden // 128):
            at = k * (hidden // 128) + c
            out[:, pl.ds(c * 128, 128)] = biases[at : at + 1]
    wait_for(all_but_one(full_p1), recv_w.at[7])
    join_pieces(full_p1, grad_w_one)

    for k, buf in ((0, gz_x), (2, gz_a)):
        wait_for(buf.at[pl.ds(0, nrow - 1)], ssem.at[k])
    for k, buf in ((0, gx_x), (2, gx_a)):
        wait_for(buf.at[pl.ds(0, nrow - 1)], ssem.at[k])
    wait_for(all_but_one(part_one), ssem.at[1])
    wait_for(all_but_one(part_two), ssem.at[3])
    wait_for(back.at[pl.ds(0, (ncol - 1) * 128)], ssem.at[4])
    for k, buf in enumerate(
        (piece_two, z_p2, piece_one, bias_z, full_p2, z_p1, bias_x, full_p1, bias_c)
    ):
        wait_for(all_but_one(buf), ssem.at[5 + k])


def hand_over(*refs):
    count = len(refs) // 2
    for src, dst in zip(refs[:count], refs[count:], strict=True):
        dst[...] = src[...]


def per_device(
    mesh_shape,
    features, upstream, tile_values, tile_rows, tile_cols, tile_count, w_one, b_one, w_two, b_two,
):
    nz, nx, ncol = mesh_shape
    nrow = nz * nx
    slots = tile_values.shape[2]
    width = features.shape[1]
    hidden = w_one.shape[1]
    ngroup = nx * ncol
    vmem = pl.BlockSpec(memory_space=pltpu.VMEM)
    anywhere = pl.BlockSpec(memory_space=pl.ANY)
    per_one = width * hidden // (8 * 128) // ngroup * 8
    per_two = hidden * hidden // (8 * 128) // ngroup * 8
    scratch = [
        pltpu.VMEM((slots + 1, 128, 128), BF),
        pltpu.VMEM((nz, ncol * 128, nx * 128), BF),
        pltpu.VMEM((nz, nx * 128, ncol * 128), BF),
        pltpu.VMEM((nrow, 96, width), BF),
        pltpu.VMEM((nrow, 32, width), BF),
        pltpu.VMEM((nrow, 96, width), BF),
        pltpu.VMEM((nrow, 32, width), BF),
        pltpu.VMEM((nz, width, nx * 128), BF),
        pltpu.VMEM((nz, nx * 128, hidden), F32),
        pltpu.VMEM((nx * 128, hidden), BF),
        pltpu.VMEM((ncol, 128, width), F32),
        pltpu.VMEM((ncol, 128, hidden), F32),
        pltpu.VMEM((ncol, 128, width), BF),
        pltpu.VMEM((ncol, 128, width), BF),
        pltpu.VMEM((ncol, 128, hidden), BF),
        pltpu.VMEM((ncol, 128, hidden), BF),
        pltpu.VMEM((ncol * 128, hidden), BF),
        pltpu.VMEM((nz // 2, nx * 128, hidden), BF),
        pltpu.VMEM((ngroup, per_one, 128), F32),
        pltpu.VMEM((ngroup, per_one, 128), F32),
        pltpu.VMEM((nz, per_one, 128), F32),
        pltpu.VMEM((ngroup, per_one, 128), F32),
        pltpu.VMEM((ngroup, per_two, 128), BF),
        pltpu.VMEM((ngroup, per_two, 128), BF),
        pltpu.VMEM((nz, per_two, 128), F32),
        pltpu.VMEM((ngroup, per_two, 128), F32),
        pltpu.VMEM((ncol, 8, 128), F32),
        pltpu.VMEM((nx, 8, 128), F32),
        pltpu.VMEM((nz, 8, 128), F32),
        pltpu.VMEM((width, hidden), F32),
        pltpu.VMEM((8, hidden), F32),
        pltpu.VMEM((128, hidden), BF),
        pltpu.VMEM((hidden // 128, 128, 128), BF),
        pltpu.VMEM((128, hidden), BF),
        pltpu.VMEM((hidden // 128, 128, hidden), F32),
        pltpu.VMEM((128, hidden), BF),
        pltpu.VMEM((width, hidden), BF),
        pltpu.VMEM((1, hidden), F32),
        pltpu.VMEM((hidden, hidden), BF),
        pltpu.VMEM((1, hidden), F32),
        pltpu.VMEM((1, slots), jnp.int32),
        pltpu.VMEM((1, slots), jnp.int32),
        pltpu.VMEM((8, ncol * nrow), jnp.int32),
        pltpu.SMEM((8, ncol * nrow), jnp.int32),
        pltpu.SemaphoreType.DMA,
        pltpu.SemaphoreType.DMA((9,)),
        pltpu.SemaphoreType.DMA((15,)),
        pltpu.SemaphoreType.DMA((2, nrow)),
        pltpu.SemaphoreType.DMA((2, nrow)),
        pltpu.SemaphoreType.DMA((2,)),
        pltpu.SemaphoreType.DMA((ncol,)),
        pltpu.SemaphoreType.DMA((9,)),
    ]
    out = pl.pallas_call(
        functools.partial(kernel, nz, nx, ncol),
        out_shape=(
            jax.ShapeDtypeStruct((128, hidden), BF),
            jax.ShapeDtypeStruct((width, hidden), F32),
            jax.ShapeDtypeStruct((1, hidden), F32),
            jax.ShapeDtypeStruct((hidden, hidden), F32),
            jax.ShapeDtypeStruct((1, hidden), F32),
        ),
        in_specs=[
            pl.BlockSpec(memory_space=pltpu.SMEM), *([anywhere] * 9),
        ],
        out_specs=(vmem,) * 5,
        scratch_shapes=scratch,
        compiler_params=pltpu.CompilerParams(
            collective_id=0, has_side_effects=True, vmem_limit_bytes=56 * 1024 * 1024
        ),
    )(
        tile_count, features, upstream, tile_values, tile_rows, tile_cols,
        w_one, b_one.reshape(1, hidden), w_two, b_two.reshape(1, hidden),
    )
    hidden_out, grad_w_one, grad_b_one, grad_w_two, grad_b_two = pl.pallas_call(
        hand_over,
        out_shape=tuple(jax.ShapeDtypeStruct(o.shape, o.dtype) for o in out),
        in_specs=[vmem] * 5,
        out_specs=(vmem,) * 5,
    )(*out)
    return (
        hidden_out, grad_w_one, grad_b_one.reshape(hidden), grad_w_two, grad_b_two.reshape(hidden)
    )


def solution(mesh, nx=4):
    nrow, ncol = mesh.shape["row"], mesh.shape["col"]
    in_specs = (
        P(("col", "row"), None),
        P(("col", "row"), None),
        P("row", "col", None, None, None),
        P("row", "col", None),
        P("row", "col", None),
        P("row", "col"),
        P(),
        P(),
        P(),
        P(),
    )
    out_specs = (P(("col", "row"), None), P(), P(), P(), P())
    return jax.shard_map(
        functools.partial(per_device, (nrow // nx, nx, ncol)),
        mesh=mesh, in_specs=in_specs, out_specs=out_specs, check_vma=False,
    )
```
